128 devices in a mesh: depth: 8 (over x_hi, y), res: 16 (over x_lo, z, core).
Axes of the slice: x: 4 (x_hi: 2, x_lo: 2; x = x_hi * 2 + x_lo), y: 4, z: 4, core: 2. Of those that a mesh axis runs over, the one named last changes fastest.
Arguments:
- family_activity: bfloat16 [2048, 16, 768], P('depth', 'res'), may hold values from -6 to 6
- rescale_factor: float32 [768], replicated, may hold values from 0.25 to 1.75
- asking_weights: bfloat16 [768, 768], P(('depth', 'res')), may hold values from -1.203125 to 1.203125
- lookup_weights: bfloat16 [768, 768], P(('depth', 'res')), may hold values from -1.203125 to 1.203125
- payload_weights: bfloat16 [768, 768], P(('depth', 'res')), may hold values from -0.21875 to 0.21875
- exit_weights: bfloat16 [768, 768], P(('depth', 'res')), may hold values from -0.625 to 0.625
- upstream_adjoint: bfloat16 [2048, 16, 768], P('depth', 'res'), may hold values from -6 to 6
Outputs:
- final_result: bfloat16 [2048, 16, 768], P('depth', 'res')
- alignment_gradient: bfloat16 [2048, 16, 768], P('depth', 'res')
- query_gradient: float32 [768, 768], P(('depth', 'res'))
- key_gradient: float32 [768, 768], P(('depth', 'res'))
- value_gradient: float32 [768, 768], P(('depth', 'res'))
- output_gradient: float32 [768, 768], P(('depth', 'res'))
- gain_gradient: float32 [768], P(('depth', 'res'))
The draws below stay inside these ranges and needn't reach their ends.
All inputs are finite; a program needn't handle non-finite values.
Results may differ from the reference program's by a relative error of at most 0.022.
The reference program's roundings to bfloat16 on the way count: a program that leaves them out, or rounds other values in their place, can miss the bound.
Values may be sent and summed in bfloat16 or wider, within the bound.
A program may use at most 128 MiB of HBM per device.

```python
import jax
import jax.numpy as jnp
from jax import lax

HEADS = 12
HEAD_DIM = 64
EMBED_SPAN = 768
HOMOLOG_TOTAL = 2048
POSITION_TOTAL = 16
N_DEPTH = 8


def draw_asking_weights(key, part):
    key = jax.random.fold_in(key, 11)
    payload_entries = jnp.clip(jax.random.normal(key, (EMBED_SPAN, EMBED_SPAN), jnp.float32), -5.0, 5.0) * (2.0 / EMBED_SPAN) ** 0.5
    return payload_entries.astype(jnp.bfloat16)


def draw_lookup_weights(key, part):
    key = jax.random.fold_in(key, 12)
    own = jnp.clip(jax.random.normal(key, (EMBED_SPAN, EMBED_SPAN), jnp.float32), -5.0, 5.0)
    payload_entries = own * (2.0 / EMBED_SPAN) ** 0.5
    return payload_entries.astype(jnp.bfloat16)


def steps_of(rng, shape, cuts, low, largest):
    def one(dim, shards_of):
        draws = jax.random.uniform(jax.random.fold_in(jax.random.fold_in(rng, 6), dim), (shards_of,), jnp.float32, low / len(cuts), largest / len(cuts))
        return jnp.repeat(jnp.exp(draws), shape[dim] // shards_of).reshape((-1,) + (1,) * (len(shape) - dim - 1))

    gain = one(*cuts[0])
    for cut in cuts[1:]:
        gain = gain * one(*cut)
    return gain


def centred(own_key, shape, deviation, limit, shards=(), kind=jnp.bfloat16):
    values = jax.random.normal(own_key, shape, jnp.float32) * deviation
    if len(shards) > 0:
        values = steps_of(own_key, shape, shards, -0.22, 0.18) * values
    return jnp.clip(values, min=-limit, max=limit).astype(kind)


def setup_inputs(seed: int = 0) -> dict:
    key_list = jax.random.split(jax.random.key(seed), 8)
    family_activity = centred(key_list[0], (HOMOLOG_TOTAL, POSITION_TOTAL, EMBED_SPAN), 1.0, 6.0, ((0, 8), (1, 16)))
    rescale_factor = jnp.clip(1.0 + 0.15 * jax.random.normal(key_list[1], (EMBED_SPAN,), jnp.float32), 0.25, 1.75)
    asking_weights = draw_asking_weights(jax.random.fold_in(key_list[7], 71), 0)
    lookup_weights = draw_lookup_weights(jax.random.fold_in(key_list[7], 71), 0)
    payload_weights = centred(key_list[4], (EMBED_SPAN, EMBED_SPAN), EMBED_SPAN ** -0.5, 0.21875, ((0, 128),))
    exit_weights = centred(key_list[5], (EMBED_SPAN, EMBED_SPAN), (EMBED_SPAN // 8) ** -0.5, 0.625, ((0, 128),))
    upstream_adjoint = centred(key_list[6], (HOMOLOG_TOTAL, POSITION_TOTAL, EMBED_SPAN), 1.0, 6.0, ((0, 8), (1, 16)))
    return dict(family_activity=family_activity, rescale_factor=rescale_factor, asking_weights=asking_weights, lookup_weights=lookup_weights, payload_weights=payload_weights, exit_weights=exit_weights, upstream_adjoint=upstream_adjoint)


def standardize_entries(family_activity, rescale_factor):
    payload_entries = family_activity.astype(jnp.float32)
    centered = payload_entries - lax.optimization_barrier(jnp.mean(payload_entries, axis=-1, keepdims=True))
    reciprocal_spread = lax.rsqrt(lax.optimization_barrier(jnp.mean(centered * centered, axis=-1, keepdims=True)) + 1e-05)
    standardized_entries = centered * reciprocal_spread
    return ((standardized_entries * rescale_factor).astype(jnp.bfloat16), standardized_entries, reciprocal_spread)

def project(rows, weight, factor):
    return (factor * jnp.dot(rows, weight, preferred_element_type=jnp.float32)).astype(jnp.bfloat16)

def to_heads(array):
    count, cols = (array.shape[0], array.shape[1])
    return jnp.transpose(array.reshape(count, cols, HEADS, HEAD_DIM), (1, 2, 0, 3)).reshape(cols * HEADS, count, HEAD_DIM)

def from_heads(array, cols):
    count = array.shape[1]
    return jnp.transpose(array.reshape(cols, HEADS, count, HEAD_DIM), (2, 0, 1, 3)).reshape(count, cols, HEADS * HEAD_DIM)

def head_pass(query, keys, payload_entries, d_att):
    scale = HEAD_DIM ** (-0.5)
    scores = jnp.dot(query, keys.T, preferred_element_type=jnp.float32)
    probs = jax.nn.softmax(scores, axis=-1)
    probs_b = probs.astype(jnp.bfloat16)
    mixed_homologs = jnp.dot(probs_b, payload_entries, preferred_element_type=jnp.float32).astype(jnp.bfloat16)
    d_probs = jnp.dot(d_att, payload_entries.T, preferred_element_type=jnp.float32)
    d_scores = probs * (d_probs - lax.optimization_barrier(jnp.sum(probs * d_probs, axis=-1, keepdims=True)))
    d_scores_b = d_scores.astype(jnp.bfloat16)
    d_query = (scale * jnp.dot(d_scores_b, keys, preferred_element_type=jnp.float32)).astype(jnp.bfloat16)
    homolog_total = query.shape[0]
    block = homolog_total // N_DEPTH
    blocks_s = d_scores_b.astype(jnp.float32).reshape(N_DEPTH, block, homolog_total)
    blocks_p = probs_b.astype(jnp.float32).reshape(N_DEPTH, block, homolog_total)
    query_blocks = query.astype(jnp.float32).reshape(N_DEPTH, block, HEAD_DIM)
    datt_blocks = d_att.astype(jnp.float32).reshape(N_DEPTH, block, HEAD_DIM)
    key_parts = jnp.einsum('jst,jsd->jtd', blocks_s, query_blocks).astype(jnp.bfloat16)
    value_parts = jnp.einsum('jst,jsd->jtd', blocks_p, datt_blocks).astype(jnp.bfloat16)
    key_parts = lax.optimization_barrier(key_parts)
    value_parts = lax.optimization_barrier(value_parts)
    d_keys = lax.optimization_barrier(jnp.sum(key_parts.astype(jnp.float32), axis=0)).astype(jnp.bfloat16)
    d_values = lax.optimization_barrier(jnp.sum(value_parts.astype(jnp.float32), axis=0)).astype(jnp.bfloat16)
    return (mixed_homologs, d_query, d_keys, d_values)

def reference(family_activity, rescale_factor, asking_weights, lookup_weights, payload_weights, exit_weights, upstream_adjoint):
    homolog_total, position_total, embed_span = family_activity.shape
    standardized_source, standardized_entries, reciprocal_spread = standardize_entries(family_activity, rescale_factor)
    query = project(standardized_source, asking_weights, HEAD_DIM ** (-0.5))
    keys = project(standardized_source, lookup_weights, 1.0)
    payload_entries = project(standardized_source, payload_weights, 1.0)
    d_att = jnp.dot(upstream_adjoint, exit_weights.T, preferred_element_type=jnp.float32).astype(jnp.bfloat16)

    def per_head(items):
        return head_pass(items[0], items[1], items[2], items[3])
    results = lax.map(per_head, (to_heads(query), to_heads(keys), to_heads(payload_entries), to_heads(d_att)))
    mixed_homologs, d_query, d_keys, d_values = [from_heads(item, position_total) for item in results]
    final_result = (family_activity.astype(jnp.float32) + jnp.dot(mixed_homologs, exit_weights, preferred_element_type=jnp.float32)).astype(jnp.bfloat16)
    rows = homolog_total * position_total
    normed_rows = standardized_source.reshape(rows, embed_span)
    query_gradient = jnp.dot(normed_rows.T, d_query.reshape(rows, embed_span), preferred_element_type=jnp.float32)
    key_gradient = jnp.dot(normed_rows.T, d_keys.reshape(rows, embed_span), preferred_element_type=jnp.float32)
    value_gradient = jnp.dot(normed_rows.T, d_values.reshape(rows, embed_span), preferred_element_type=jnp.float32)
    output_gradient = jnp.dot(mixed_homologs.reshape(rows, embed_span).T, upstream_adjoint.reshape(rows, embed_span), preferred_element_type=jnp.float32)
    d_normed = jnp.dot(d_query, asking_weights.T, preferred_element_type=jnp.float32)
    d_normed = d_normed + jnp.dot(d_keys, lookup_weights.T, preferred_element_type=jnp.float32)
    d_normed = d_normed + jnp.dot(d_values, payload_weights.T, preferred_element_type=jnp.float32)
    gain_gradient = lax.optimization_barrier(jnp.sum((d_normed * standardized_entries).reshape(rows, embed_span), axis=0))
    unit_gradient = d_normed * rescale_factor
    alignment_gradient = upstream_adjoint.astype(jnp.float32) + reciprocal_spread * (unit_gradient - lax.optimization_barrier(jnp.mean(unit_gradient, axis=-1, keepdims=True)) - standardized_entries * lax.optimization_barrier(jnp.mean(unit_gradient * standardized_entries, axis=-1, keepdims=True)))
    return (final_result, alignment_gradient.astype(jnp.bfloat16), query_gradient, key_gradient, value_gradient, output_gradient, gain_gradient)
```

```python
import jax
import jax.numpy as jnp
from jax import lax
from jax.experimental import pallas as pl
from jax.experimental.pallas import tpu as pltpu
from jax.sharding import PartitionSpec as P

HEADS = 12
HD = 64
E = 768
ND = 8
NR = 16
ROWS = 256
SEQ = ND * ROWS
SCALE = HD ** (-0.5)
MESH = pl.DeviceIdType.MESH
BF = jnp.bfloat16
F32 = jnp.float32
VMEM_LIMIT = 56 * 1024 * 1024


def place():
    d = lax.axis_index("depth")
    r = lax.axis_index("res")
    return d, r, d // 4, d % 4, r // 8, (r // 2) % 4, r % 2


def at(d, r):
    return {"depth": d, "res": r}


def barrier(peers):
    sem = pltpu.get_barrier_semaphore()
    for peer in peers:
        pl.semaphore_signal(sem, inc=1, device_id=peer, device_id_type=MESH)
    pl.semaphore_wait(sem, len(peers))


def remote(src, dst, send, recv, peer):
    return pltpu.make_async_remote_copy(
        src_ref=src, dst_ref=dst, send_sem=send, recv_sem=recv, device_id=peer, device_id_type=MESH
    )


def dot(a, b, dims):
    return lax.dot_general(a, b, ((dims[0], dims[1]), ((), ())), preferred_element_type=F32)


def gather_kernel(n_ref, u_ref, w_ref, n_all, u_all, w_all, ns, nr, us, ur, ws, wr, loc):
    d, r, xh, y, xl, z, core = place()
    zc = z * 2 + core
    depth_peers = [at((d + s) % ND, r) for s in range(1, ND)]
    y_peers = [at(xh * 4 + (y + s) % 4, r) for s in range(1, 4)]
    x_peers = [at((1 - xh) * 4 + y, r), at(d, (1 - xl) * 8 + zc), at((1 - xh) * 4 + y, (1 - xl) * 8 + zc)]
    z_peers = [at(d, xl * 8 + ((z + s) % 4) * 2 + core) for s in range(1, 4)]
    c_peer = at(d, xl * 8 + z * 2 + 1 - core)
    barrier(depth_peers + x_peers[1:] + z_peers + [c_peer])

    own = [
        pltpu.make_async_copy(n_ref, n_all.at[d], loc.at[0]),
        pltpu.make_async_copy(u_ref, u_all.at[d], loc.at[1]),
        pltpu.make_async_copy(w_ref, w_all.at[xh, y, xl, zc], loc.at[2]),
    ]
    for c in own:
        c.start()
    cy = [remote(w_ref, w_all.at[xh, y, xl, zc], ws.at[s], wr.at[s], y_peers[s]) for s in range(3)]
    for c in cy:
        c.start()
    cn = [remote(n_ref, n_all.at[d], ns.at[s], nr.at[s], depth_peers[s]) for s in range(7)]
    for c in cn:
        c.start()
    own[2].wait()
    for c in cy:
        c.wait()
    slab = w_all.at[xh, :, xl, zc]
    cx = [remote(slab, slab, ws.at[3 + s], wr.at[3 + s], x_peers[s]) for s in range(3)]
    for c in cx:
        c.start()
    for c in cx:
        c.wait()
    slab = w_all.at[:, :, :, zc]
    cz = [remote(slab, slab, ws.at[6 + s], wr.at[6 + s], z_peers[s]) for s in range(3)]
    for c in cz:
        c.start()
    cc = [remote(slab, slab, ws.at[9], wr.at[9], c_peer)]
    cc[0].start()
    cu = [remote(u_ref, u_all.at[d], us.at[s], ur.at[s], depth_peers[s]) for s in range(7)]
    for c in cu:
        c.start()
    for s in range(3):
        cz[s].wait()
        there = w_all.at[:, :, :, ((z + 3 - s) % 4) * 2 + core]
        c = remote(there, there, ws.at[10 + s], wr.at[10 + s], c_peer)
        c.start()
        cc.append(c)
    for c in cc + cn + cu:
        c.wait()
    own[0].wait()
    own[1].wait()


def gather(normed, upstream, shard):
    any_spec = pl.BlockSpec(memory_space=pl.ANY)
    return pl.pallas_call(
        gather_kernel,
        out_shape=(
            jax.ShapeDtypeStruct((ND, ROWS, E), BF),
            jax.ShapeDtypeStruct((ND, ROWS, E), BF),
            jax.ShapeDtypeStruct((2, 4, 2, 8, 24, E), BF),
        ),
        in_specs=[any_spec] * 3,
        out_specs=(any_spec,) * 3,
        scratch_shapes=[
            pltpu.SemaphoreType.DMA((7,)),
            pltpu.SemaphoreType.DMA((7,)),
            pltpu.SemaphoreType.DMA((7,)),
            pltpu.SemaphoreType.DMA((7,)),
            pltpu.SemaphoreType.DMA((13,)),
            pltpu.SemaphoreType.DMA((13,)),
            pltpu.SemaphoreType.DMA((3,)),
        ],
        compiler_params=pltpu.CompilerParams(collective_id=1, has_side_effects=True),
        name="gather",
    )(normed, upstream, shard)


def attention_kernel(
    n_ref, u_ref, wq_ref, wk_ref, wv_ref, we_ref, p_ref, rs_ref,
    q_s, k_s, v_s, a_s, kt_s, vt_s, dk_s, dv_s, gq_s, go_s, gt_s,
):
    d, r, xh, y, xl, z, core = place()
    par = d % 2

    def project(c, _):
        rows = pl.ds(c * ROWS, ROWS)
        n = n_ref[c]
        q = (SCALE * dot(n, wq_ref[...], ((1,), (0,)))).astype(BF)
        k = dot(n, wk_ref[...], ((1,), (0,))).astype(BF)
        v = dot(n, wv_ref[...], ((1,), (0,))).astype(BF)
        a = dot(u_ref[c], we_ref[...], ((1,), (1,))).astype(BF)
        for h in range(2):
            cols = slice(h * HD, h * HD + HD)
            q_s[h, rows, :] = q[:, cols]
            k_s[h, rows, :] = k[:, cols]
            v_s[h, rows, :] = v[:, cols]
            a_s[h, rows, :] = a[:, cols]
        kt = k.T
        vt = v.T
        for h in range(2):
            rws = slice(h * HD, h * HD + HD)
            kt_s[h, c] = kt[rws]
            vt_s[h, c] = vt[rws]
        return 0

    lax.fori_loop(0, ND, project, 0)
    dk_s[...] = jnp.zeros_like(dk_s)
    dv_s[...] = jnp.zeros_like(dv_s)
    gq_s[...] = jnp.zeros_like(gq_s)
    go_s[...] = jnp.zeros_like(go_s)

    def step(i, _):
        h = i // 8
        c = jnp.where(h == 0, i, i - 8 + 4 * par)
        rows = pl.ds(pl.multiple_of(c * ROWS, ROWS), ROWS)
        q = q_s[h, rows, :]
        a = a_s[h, rows, :]
        st = dot(k_s[h], q, ((1,), (1,)))
        m = jnp.max(st, axis=0, keepdims=True)
        e = jnp.exp(st - m)
        p = e * (1.0 / jnp.sum(e, axis=0, keepdims=True))
        pb = p.astype(BF)
        dp = dot(v_s[h], a, ((1,), (1,)))
        delta = jnp.sum(p * dp, axis=0, keepdims=True)
        ds = (p * (dp - delta)).astype(BF)
        att = jnp.zeros((HD, ROWS), F32)
        dq = jnp.zeros((HD, ROWS), F32)
        for t in range(ND):
            ts = slice(t * ROWS, t * ROWS + ROWS)
            att += dot(vt_s[h, t], pb[ts], ((1,), (0,)))
            dq += dot(kt_s[h, t], ds[ts], ((1,), (0,)))
        att = att.astype(BF)
        dq = (SCALE * dq).astype(BF)
        dk_s[h] += dot(ds, q, ((1,), (0,)))
        dv_s[h] += dot(pb, a, ((1,), (0,)))
        go_s[h] += dot(att, u_ref[c], ((1,), (0,)))
        gq_s[h] += dot(dq, n_ref[c], ((1,), (0,)))
        base = pl.multiple_of(h * 384, 128)
        p_ref[c, pl.ds(base, HD), :] = att
        p_ref[c, pl.ds(base + HD, HD), :] = dq
        return 0

    lax.fori_loop(0, 12, step, 0)

    def finish(c, carry):
        rows = pl.ds(pl.multiple_of(c * ROWS, ROWS), ROWS)
        n = n_ref[c]
        out = []
        for h in range(2):
            dkt = dk_s[h, rows, :].T.astype(BF)
            dvt = dv_s[h, rows, :].T.astype(BF)
            p_ref[c, 128 + 128 * h:192 + 128 * h, :] = dkt
            p_ref[c, 192 + 128 * h:256 + 128 * h, :] = dvt
            gt_s[128 + h * HD:192 + h * HD] += dot(dkt, n, ((1,), (0,)))
            gt_s[256 + h * HD:320 + h * HD] += dot(dvt, n, ((1,), (0,)))
        return carry

    gt_s[...] = jnp.zeros_like(gt_s)
    lax.fori_loop(0, ND, finish, 0)
    gt_s[0:64] = gq_s[0]
    gt_s[64:128] = gq_s[1]
    gt = gt_s[...].astype(BF)
    go = jnp.concatenate([go_s[0], go_s[1]], axis=0).astype(BF)

    def order(b, _):
        R = lax.broadcasted_iota(jnp.int32, (256, E), 0) + b * 256
        F = lax.broadcasted_iota(jnp.int32, (256, E), 1)
        i = R % 8
        hit = (F == 6 * (16 * ((R // 8) % 8) + R // 64) + i) & (i < 6)
        hot = jnp.where(hit, 1.0, 0.0).astype(BF)
        g = dot(hot, gt, ((1,), (1,))).astype(BF)
        for s in range(4):
            rs_ref[4 * b + s, 0:64, :] = g[64 * s:64 * s + 64]
        return 0

    lax.fori_loop(0, 4, order, 0)
    R = lax.broadcasted_iota(jnp.int32, (256, 128), 0)
    C = lax.broadcasted_iota(jnp.int32, (256, 128), 1)
    i = R % 8
    feature = jnp.where(C < 64, C + 128 * par, C)
    hit = (feature == 96 * ((R // 8) % 2) + 6 * (R // 16) + i) & (i < 6)
    hot = jnp.where(hit, 1.0, 0.0).astype(BF)
    g = dot(hot, go, ((1,), (0,))).astype(BF)
    for s in range(NR):
        rs_ref[s, 64:80, :] = g[16 * s:16 * s + 16, 0:384]
        rs_ref[s, 80:96, :] = g[16 * s:16 * s + 16, 384:768]


def attention(n_all, u_all, wq, wk, wv, we):
    vm = pl.BlockSpec(memory_space=pltpu.VMEM)
    return pl.pallas_call(
        attention_kernel,
        out_shape=(
            jax.ShapeDtypeStruct((ND, 512, ROWS), BF),
            jax.ShapeDtypeStruct((NR, 96, 384), BF),
        ),
        in_specs=[vm] * 6,
        out_specs=(vm, vm),
        scratch_shapes=[pltpu.VMEM((2, SEQ, HD), BF)] * 4
        + [pltpu.VMEM((2, ND, HD, ROWS), BF)] * 2
        + [pltpu.VMEM((2, SEQ, HD), F32)] * 2
        + [pltpu.VMEM((2, HD, E), F32)] * 2
        + [pltpu.VMEM((384, E), F32)],
        compiler_params=pltpu.CompilerParams(vmem_limit_bytes=VMEM_LIMIT),
        name="attention",
    )(n_all, u_all, wq, wk, wv, we)


def exchange_kernel(
    p_ref, rs_ref, b_ref, fin_ref,
    bc, acc1, bz, acc2, bx, acc3, finq, fino, ps, pr, hs, hr, gs, gr, loc,
):
    d, r, xh, y, xl, z, core = place()
    par = d % 2
    zc = z * 2 + core
    depth_peers = [at((d + s) % ND, r) for s in range(1, ND)]
    z_peers = [at(d, xl * 8 + ((z + s) % 4) * 2 + core) for s in range(1, 4)]
    x_peer = at(d, (1 - xl) * 8 + zc)
    c_peer = at(d, xl * 8 + z * 2 + 1 - core)
    barrier(depth_peers + z_peers + [x_peer, c_peer])

    local = pltpu.make_async_copy(p_ref.at[d], b_ref.at[d], loc.at[0])
    local.start()
    cc = []
    for g in range(8):
        c = remote(rs_ref.at[2 * g + 1 - core], bc.at[g], gs.at[g], gr.at[g], c_peer)
        c.start()
        cc.append(c)
    cp = []
    for s in range(1, ND):
        to = (d + s) % ND
        c = remote(p_ref.at[to, 0:384], b_ref.at[d, 0:384], ps.at[s - 1], pr.at[s - 1], depth_peers[s - 1])
        c.start()
        cp.append(c)
    ch = []
    for s in range(1, ND):
        to = (d + s) % ND
        c = remote(p_ref.at[to, 384:512], b_ref.at[d, 384:512], hs.at[s - 1], hr.at[s - 1], depth_peers[s - 1])
        pl.when(to // 4 == par)(c.start)
        ch.append(c)
    for g in range(8):
        cc[g].wait()
        acc1[g] = (rs_ref[2 * g + core].astype(F32) + bc[g].astype(F32)).astype(BF)
    cz = []
    for s in range(1, 4):
        to = (z + s) % 4
        for x in range(2):
            k = (s - 1) * 2 + x
            c = remote(acc1.at[x * 4 + to], bz.at[s - 1, x], gs.at[8 + k], gr.at[8 + k], z_peers[s - 1])
            c.start()
            cz.append(c)
    for c in cz:
        c.wait()
    total = [
        acc1[x * 4 + z].astype(F32) + bz[0, x].astype(F32) + bz[1, x].astype(F32) + bz[2, x].astype(F32)
        for x in range(2)
    ]
    acc2[0] = total[0].astype(BF)
    acc2[1] = total[1].astype(BF)
    cx = remote(acc2.at[1 - xl], bx, gs.at[14], gr.at[14], x_peer)
    cx.start()
    cx.wait()
    acc3[...] = acc2[xl].astype(F32) + bx[...].astype(F32)
    last = []
    for s in range(1, ND):
        to = (d + s) % ND
        rows = pl.ds(pl.multiple_of(to * 8, 8), 8)
        c = remote(acc3.at[rows], finq.at[d], gs.at[14 + s], gr.at[14 + s], depth_peers[s - 1])
        c.start()
        last.append(c)
    partner = at(d + 1 - 2 * par, r)
    for half in range(2):
        rows = pl.ds(pl.multiple_of(64 + half * 16 + (1 - par) * 8, 8), 8)
        c = remote(acc3.at[rows], fino.at[half], gs.at[22 + half], gr.at[22 + half], partner)
        c.start()
        last.append(c)
    finq[d] = acc3[pl.ds(pl.multiple_of(d * 8, 8), 8), :]
    for c in last:
        c.wait()
    for j in range(4):
        for m in range(3):
            one = finq[2 * j, :, m * 128:m * 128 + 128]
            two = finq[2 * j + 1, :, m * 128:m * 128 + 128]
            fin_ref[m, :, 192 * j:192 * j + 192] = jnp.concatenate(
                [one[:, 0:64], one[:, 64:128] + two[:, 64:128], two[:, 0:64]], axis=1
            )
    for half in range(2):
        rows = pl.ds(pl.multiple_of(64 + half * 16 + par * 8, 8), 8)
        fin_ref[3, :, half * 384:half * 384 + 384] = acc3[rows, :] + fino[half]
    local.wait()
    for c in cp:
        c.wait()
    for s in range(1, ND):
        to = (d + s) % ND
        came = (d + ND - s) % ND
        pl.when(to // 4 == par)(ch[s - 1].wait_send)
        pl.when(came % 2 == d // 4)(ch[s - 1].wait_recv)


def exchange(p, rs):
    vm = pl.BlockSpec(memory_space=pltpu.VMEM)
    return pl.pallas_call(
        exchange_kernel,
        out_shape=(
            jax.ShapeDtypeStruct((ND, 512, ROWS), BF),
            jax.ShapeDtypeStruct((4, 8, E), F32),
        ),
        in_specs=[vm, vm],
        out_specs=(vm, vm),
        scratch_shapes=[
            pltpu.VMEM((8, 96, 384), BF),
            pltpu.VMEM((8, 96, 384), BF),
            pltpu.VMEM((3, 2, 96, 384), BF),
            pltpu.VMEM((2, 96, 384), BF),
            pltpu.VMEM((96, 384), BF),
            pltpu.VMEM((96, 384), F32),
            pltpu.VMEM((ND, 8, 384), F32),
            pltpu.VMEM((2, 8, 384), F32),
            pltpu.SemaphoreType.DMA((7,)),
            pltpu.SemaphoreType.DMA((7,)),
            pltpu.SemaphoreType.DMA((7,)),
            pltpu.SemaphoreType.DMA((7,)),
            pltpu.SemaphoreType.DMA((24,)),
            pltpu.SemaphoreType.DMA((24,)),
            pltpu.SemaphoreType.DMA((1,)),
        ],
        compiler_params=pltpu.CompilerParams(
            collective_id=2, has_side_effects=True, vmem_limit_bytes=VMEM_LIMIT
        ),
        name="exchange",
    )(p, rs)


def rows_kernel(b_ref, x_ref, u_ref, gain_ref, wq_ref, wk_ref, wv_ref, we_ref, out_ref, al_ref, t_s):
    half = lax.axis_index("depth") // 4
    for j in range(4):
        lo, hi = 2 * j, 2 * j + 1
        sh = 2 * j + half
        for m in range(4):
            t_s[m, 192 * j:192 * j + 64] = b_ref[lo, 64 * m:64 * m + 64]
            t_s[m, 192 * j + 128:192 * j + 192] = b_ref[hi, 64 * m:64 * m + 64]
        for m in range(2):
            t_s[m, 192 * j + 64:192 * j + 128] = b_ref[sh, 384 + 64 * m:448 + 64 * m]
            rows = slice(256 + 64 * m, 320 + 64 * m)
            t_s[2 + m, 192 * j + 64:192 * j + 128] = (
                b_ref[lo, rows].astype(F32) + b_ref[hi, rows].astype(F32)
            ).astype(BF)
    x = x_ref[...].astype(F32)
    att = t_s[0].T
    out_ref[...] = (x + dot(att, we_ref[...], ((1,), (0,)))).astype(BF)
    dn = dot(t_s[1].T, wq_ref[...], ((1,), (1,)))
    dn += dot(t_s[2].T, wk_ref[...], ((1,), (1,)))
    dn += dot(t_s[3].T, wv_ref[...], ((1,), (1,)))
    centered = x - jnp.mean(x, axis=-1, keepdims=True)
    inverse = lax.rsqrt(jnp.mean(centered * centered, axis=-1, keepdims=True) + 1e-05)
    unit = centered * inverse
    du = dn * gain_ref[...]
    al_ref[...] = (
        u_ref[...].astype(F32)
        + inverse
        * (du - jnp.mean(du, axis=-1, keepdims=True) - unit * jnp.mean(du * unit, axis=-1, keepdims=True))
    ).astype(BF)


def rows_results(back, x, u, gain, wq, wk, wv, we):
    vm = pl.BlockSpec(memory_space=pltpu.VMEM)
    return pl.pallas_call(
        rows_kernel,
        out_shape=(jax.ShapeDtypeStruct((ROWS, E), BF), jax.ShapeDtypeStruct((ROWS, E), BF)),
        in_specs=[vm] * 8,
        out_specs=(vm, vm),
        scratch_shapes=[pltpu.VMEM((4, E, ROWS), BF)],
        compiler_params=pltpu.CompilerParams(vmem_limit_bytes=VMEM_LIMIT),
        name="rows",
    )(back, x, u, gain, wq, wk, wv, we)


def body(x, gain, wq, wk, wv, we, u):
    x = x.reshape(ROWS, E)
    u = u.reshape(ROWS, E)
    xf = x.astype(F32)
    centered = xf - jnp.mean(xf, axis=-1, keepdims=True)
    inverse = lax.rsqrt(jnp.mean(centered * centered, axis=-1, keepdims=True) + 1e-05)
    normed = (centered * inverse * gain).astype(BF)
    shard = jnp.concatenate([wq, wk, wv, we], axis=0)
    n_all, u_all, w_all = gather(normed, u, shard)
    w_full = w_all.reshape(128, 4, 6, E).transpose(1, 0, 2, 3).reshape(4, E, E)
    d = lax.axis_index("depth")
    r = lax.axis_index("res")
    j, par = d // 2, d % 2

    def columns(w):
        three = lax.dynamic_slice(w, (0, 192 * j), (E, 192))
        return jnp.concatenate(
            [jnp.where(par == 0, three[:, 0:64], three[:, 128:192]), three[:, 64:128]], axis=1
        )

    three = lax.dynamic_slice(w_full[3], (192 * j, 0), (192, E))
    we_own = jnp.concatenate([jnp.where(par == 0, three[0:64], three[128:192]), three[64:128]], axis=0)
    p, rs = attention(n_all, u_all, columns(w_full[0]), columns(w_full[1]), columns(w_full[2]), we_own)
    back, fin = exchange(p, rs)
    out, al = rows_results(
        back, x, u, gain.reshape(1, E), w_full[0], w_full[1], w_full[2], w_full[3]
    )
    gq, gk, gv, go = fin[0, :6], fin[1, :6], fin[2, :6], fin[3, :6]
    own_gain = lax.dynamic_slice(gain, (6 * (NR * d + r),), (6,))
    dgain = (
        jnp.sum(gq * wq.astype(F32) + gk * wk.astype(F32) + gv * wv.astype(F32), axis=1) / own_gain
    )
    return out.reshape(ROWS, 1, E), al.reshape(ROWS, 1, E), gq, gk, gv, go, dgain


def solution(mesh):
    rows = P("depth", "res", None)
    shard = P(("depth", "res"), None)
    return jax.shard_map(
        body,
        mesh=mesh,
        in_specs=(rows, P(), shard, shard, shard, shard, rows),
        out_specs=(rows, rows, shard, shard, shard, shard, P(("depth", "res"))),
        check_vma=False,
    )
```

```python
import jax
import jax.numpy as jnp
from jax import lax
from jax.experimental import pallas as pl
from jax.experimental.pallas import tpu as pltpu
from jax.sharding import PartitionSpec as P

HD = 64
E = 768
ND = 8
NR = 16
ROWS = 256
SEQ = ND * ROWS
TILE = 256
SCALE = HD ** (-0.5)
MESH = pl.DeviceIdType.MESH
BF = jnp.bfloat16
F32 = jnp.float32
VMEM_LIMIT = 58 * 1024 * 1024


def place():
    d = lax.axis_index("depth")
    r = lax.axis_index("res")
    return d, r, d // 4, d % 4, r // 8, (r // 2) % 4, r % 2


def at(d, r):
    return {"depth": d, "res": r}


def barrier(peers):
    sem = pltpu.get_barrier_semaphore()
    for peer in peers:
        pl.semaphore_signal(sem, inc=1, device_id=peer, device_id_type=MESH)
    pl.semaphore_wait(sem, len(peers))


def remote(src, dst, send, recv, peer):
    return pltpu.make_async_remote_copy(
        src_ref=src, dst_ref=dst, send_sem=send, recv_sem=recv, device_id=peer, device_id_type=MESH
    )


def start(copies):
    for c in copies:
        c.start()


def wait(copies):
    for c in copies:
        c.wait()


def dot(a, b, ca, cb):
    return lax.dot_general(a, b, (((ca,), (cb,)), ((), ())), preferred_element_type=F32)


def hot(mask):
    return jnp.where(mask, 1.0, 0.0).astype(BF)


def moved(a, b, ca, cb):
    return dot(a, b, ca, cb).astype(BF)


def ring(src, full, d, xh, y, r, ss, rs):
    e = (d + 4) % ND
    up, down = at(xh * 4 + (y + 1) % 4, r), at(xh * 4 + (y + 3) % 4, r)
    lo, hi = xh * 4 + (y + 3) % 4, xh * 4 + (y + 1) % 4
    lo2, hi2 = (lo + 4) % ND, (hi + 4) % ND

    def near(k, peer, block, k0):
        return remote(block, k, ss.at[k0], rs.at[k0], peer)

    c0 = near(full.at[d], at(e, r), src, 0)
    a = near(full.at[d], up, src, 1)
    b = near(full.at[d], down, src, 2)
    a2 = near(full.at[e], up, full.at[e], 3)
    b2 = near(full.at[e], down, full.at[e], 4)
    f1 = near(full.at[lo, 0:128], up, full.at[lo, 0:128], 5)
    f2 = near(full.at[hi, 128:256], down, full.at[hi, 128:256], 6)
    g1 = near(full.at[lo2, 0:128], up, full.at[lo2, 0:128], 7)
    g2 = near(full.at[hi2, 128:256], down, full.at[hi2, 128:256], 8)
    return c0, (a, b), (a2, b2), (f1, f2), (g1, g2)


def kernel(
    x_ref, u_ref, gain_ref, wq_ref, wk_ref, wv_ref, we_ref,
    out_ref, al_ref, gq_ref, gk_ref, gv_ref, go_ref, dg_ref,
    n_all, u_all, wl, wr, wc, w_full, hot_s, sel_s,
    q_s, k_s, v_s, a_s, kt_s, vt_s, a_out, a_in, lse_s, p_s, dp_s, dk_s, dv_s,
    p_buf, b_buf, gt_s, ga_s, rs, bc, acc1, bz, acc2, bx, acc3, finq, fino, t_s,
    ns, nr, us, ur, ws, wrs, as_, ar, ps, pr, gs, gr, loc,
):
    d, r, xh, y, xl, z, core = place()
    par, j, half = d % 2, d // 2, d // 4
    zc = z * 2 + core
    depth_peers = [at((d + s) % ND, r) for s in range(1, ND)]
    y_peers = [at(xh * 4 + (y + s) % 4, r) for s in range(1, 4)]
    x_peers = [at((1 - xh) * 4 + y, r), at(d, (1 - xl) * 8 + zc), at((1 - xh) * 4 + y, (1 - xl) * 8 + zc)]
    z_peers = [at(d, xl * 8 + ((z + s) % 4) * 2 + core) for s in range(1, 4)]
    z_from = [((z + 4 - s) % 4) * 2 + core for s in range(1, 4)]
    c_peer = at(d, xl * 8 + z * 2 + 1 - core)
    barrier(depth_peers + x_peers[1:] + z_peers + [c_peer])

    top = jnp.concatenate(
        [wq_ref[...].astype(F32), wk_ref[...].astype(F32), wv_ref[0:4].astype(F32)], axis=0
    )
    rest = jnp.concatenate([wv_ref[4:6].astype(F32), we_ref[...].astype(F32)], axis=0)
    rest = jnp.concatenate([rest[:, 0:384], rest[:, 384:768]], axis=0)
    wl[xh, y, xl, zc] = top.astype(BF)
    wr[xh, y, xl, zc] = rest.astype(BF)
    wy = []
    for s in range(3):
        for k, w in enumerate((wl, wr)):
            one = w.at[xh, y, xl, zc]
            wy.append(remote(one, one, ws.at[2 * s + k], wrs.at[2 * s + k], y_peers[s]))
    start(wy)

    x = x_ref[...].astype(F32)
    centered = x - jnp.mean(x, axis=-1, keepdims=True)
    inverse = lax.rsqrt(jnp.mean(centered * centered, axis=-1, keepdims=True) + 1e-05)
    n_all[d] = (centered * inverse * gain_ref[...]).astype(BF)
    n0, n1, n2, n3, n4 = ring(n_all.at[d], n_all, d, xh, y, r, ns, nr)
    n0.start()
    start(n1)
    own_u = pltpu.make_async_copy(u_ref, u_all.at[d], loc.at[0])
    own_u.start()

    window = pl.multiple_of(128 * ((3 * j) // 2), 128)
    offset = 192 * j - 128 * ((3 * j) // 2)
    R = lax.broadcasted_iota(jnp.int32, (96, 256), 0)
    K = lax.broadcasted_iota(jnp.int32, (96, 256), 1)
    o16, i6 = 16 * (R // 6), R % 6
    hot_s[0] = hot(K == o16 + i6)
    hot_s[1] = hot(K == o16 + 6 + i6)
    hot_s[2] = hot((K == o16 + 12 + i6) & (i6 < 4))
    hot_s[3] = hot((K == o16 + i6 - 4) & (i6 >= 4))
    hot_s[4] = hot((K == o16 + 8 + i6 - 4) & (i6 >= 4))
    hot_s[5] = hot(K == o16 + 2 + i6)
    hot_s[6] = hot(K == o16 + 10 + i6)
    K2 = lax.broadcasted_iota(jnp.int32, (256, 128), 0)
    C2 = lax.broadcasted_iota(jnp.int32, (256, 128), 1)
    pick = hot(K2 == jnp.where(C2 < 64, offset + 128 * par + C2, offset + C2))
    p_buf[:, 384:512, :] = jnp.zeros((ND, 128, ROWS), BF)

    wait(wy)
    wx = []
    for s in range(3):
        for k, w in enumerate((wl, wr)):
            slab = w.at[xh, :, xl, zc]
            wx.append(remote(slab, slab, ws.at[6 + 2 * s + k], wrs.at[6 + 2 * s + k], x_peers[s]))
    start(wx)
    n0.wait()
    start(n2)
    wait(n1)
    start(n3)
    wait(wx)

    mine = wl.at[:, :, :, zc, :, pl.ds(window, 256)]
    wz1 = [remote(mine, wc.at[:, :, :, zc], ws.at[12 + s], wrs.at[12 + s], z_peers[s]) for s in range(3)]
    start(wz1)
    wc1 = [remote(mine, wc.at[:, :, :, zc], ws.at[15], wrs.at[15], c_peer)]
    start(wc1)
    own_w = pltpu.make_async_copy(mine, wc.at[:, :, :, zc], loc.at[1])
    own_w.start()
    slab = wr.at[:, :, :, zc]
    wz2 = [remote(slab, slab, ws.at[19 + s], wrs.at[19 + s], z_peers[s]) for s in range(3)]
    start(wz2)
    wc2 = [remote(slab, slab, ws.at[22], wrs.at[22], c_peer)]
    start(wc2)
    for s in range(3):
        wz1[s].wait()
        there = wc.at[:, :, :, z_from[s]]
        c = remote(there, there, ws.at[16 + s], wrs.at[16 + s], c_peer)
        c.start()
        wc1.append(c)
    wait(n2)
    start(n4)
    slab = wl.at[:, :, :, zc]
    wz3 = [remote(slab, slab, ws.at[26 + s], wrs.at[26 + s], z_peers[s]) for s in range(3)]
    start(wz3)
    wc3 = [remote(slab, slab, ws.at[29], wrs.at[29], c_peer)]
    start(wc3)
    wait(wc1)
    own_w.wait()

    for g in range(8):
        s1 = moved(wc[g // 4, g % 4].reshape(256, 256), pick, 1, 0)
        rows = slice(96 * g, 96 * g + 96)
        sel_s[0, rows] = moved(hot_s[0], s1, 1, 0)
        sel_s[1, rows] = moved(hot_s[1], s1, 1, 0)
        sel_s[2, rows] = moved(hot_s[2], s1, 1, 0)
    wait(n3)
    wait(n4)

    def project_qk(c, _):
        rows = pl.ds(pl.multiple_of(c * ROWS, ROWS), ROWS)
        n = n_all[c]
        q = (SCALE * dot(n, sel_s[0], 1, 0)).astype(BF)
        k = dot(n, sel_s[1], 1, 0).astype(BF)
        kt = k.T
        for h in range(2):
            q_s[h, rows, :] = q[:, h * HD:h * HD + HD]
            k_s[h, rows, :] = k[:, h * HD:h * HD + HD]
            kt_s[h, c] = kt[h * HD:h * HD + HD]
        return 0

    lax.fori_loop(0, ND, project_qk, 0)

    def stats(h, c):
        q = q_s[h, pl.ds(pl.multiple_of(c * ROWS, ROWS), ROWS), :]
        m = jnp.full((8, ROWS), -jnp.inf, F32)
        l = jnp.zeros((8, ROWS), F32)
        for t in range(SEQ // TILE):
            s = dot(k_s[h, t * TILE:t * TILE + TILE, :], q, 1, 1).reshape(TILE // 8, 8, ROWS)
            new = jnp.maximum(m, jnp.max(s, axis=0))
            l = l * jnp.exp(m - new) + jnp.sum(jnp.exp(s - new[None]), axis=0)
            m = new
        top = jnp.max(m, axis=0, keepdims=True)
        lse_s[h, c] = top + jnp.log(jnp.sum(l * jnp.exp(m - top), axis=0, keepdims=True))

    def stats_shared(i, _):
        stats(1, 4 * par + i)
        return 0

    def stats_own(i, _):
        stats(0, i)
        return 0

    for s in range(3):
        wz2[s].wait()
        there = wr.at[:, :, :, z_from[s]]
        c = remote(there, there, ws.at[23 + s], wrs.at[23 + s], c_peer)
        c.start()
        wc2.append(c)
    lax.fori_loop(0, 4, stats_shared, 0)
    wait(wc2)

    for g in range(8):
        s2 = wr[g // 4, g % 4].reshape(256, 384)
        rows = slice(96 * g, 96 * g + 96)
        w_full[3, rows, 0:384] = moved(hot_s[5], s2, 1, 0)
        w_full[3, rows, 384:768] = moved(hot_s[6], s2, 1, 0)
    a = dot(u_ref[...], w_full[3], 1, 1).astype(BF)
    for t in range(ND):
        own, sh = 192 * (t // 2) + 128 * (t % 2), 192 * (t // 2) + 64
        a_out[t] = jnp.concatenate([a[:, own:own + HD], a[:, sh:sh + HD]], axis=1)
    ca = []
    for s in range(1, ND):
        c = remote(a_out.at[(d + s) % ND], a_in.at[d], as_.at[s - 1], ar.at[s - 1], depth_peers[s - 1])
        c.start()
        ca.append(c)
    u0, u1, u2, u3, u4 = ring(u_ref, u_all, d, xh, y, r, us, ur)
    u0.start()
    start(u1)
    a_in[d] = a_out[d]

    inner = pl.multiple_of(128 * ((3 * j) // 2) - 384 * half, 128)
    for g in range(8):
        s2 = moved(wr[g // 4, g % 4, :, :, :, pl.ds(inner, 256)].reshape(256, 256), pick, 1, 0)
        late = jnp.where(half == 0, hot_s[3], hot_s[4])
        rows = slice(96 * g, 96 * g + 96)
        sel_s[2, rows] = sel_s[2, rows] + moved(late, s2, 1, 0)

    def project_v(c, _):
        rows = pl.ds(pl.multiple_of(c * ROWS, ROWS), ROWS)
        v = dot(n_all[c], sel_s[2], 1, 0).astype(BF)
        vt = v.T
        for h in range(2):
            v_s[h, rows, :] = v[:, h * HD:h * HD + HD]
            vt_s[h, c] = vt[h * HD:h * HD + HD]
        return 0

    lax.fori_loop(0, ND, project_v, 0)
    lax.fori_loop(0, 8, stats_own, 0)
    wait(ca)

    def spread(c, _):
        rows = pl.ds(pl.multiple_of(c * ROWS, ROWS), ROWS)
        got = a_in[c]
        a_s[0, rows, :] = got[:, 0:HD]
        a_s[1, rows, :] = got[:, HD:2 * HD]
        return 0

    lax.fori_loop(0, ND, spread, 0)
    u0.wait()
    start(u2)
    wait(u1)
    start(u3)
    for s in range(3):
        wz3[s].wait()
        there = wl.at[:, :, :, z_from[s]]
        c = remote(there, there, ws.at[30 + s], wrs.at[30 + s], c_peer)
        c.start()
        wc3.append(c)

    def attend(h, c, base):
        rows = pl.ds(pl.multiple_of(c * ROWS, ROWS), ROWS)
        q = q_s[h, rows, :]
        a = a_s[h, rows, :]
        qt, at_ = q.T, a.T
        lse = lse_s[h, c]
        delta = jnp.zeros((8, ROWS), F32)
        for t in range(SEQ // TILE):
            ts = slice(t * TILE, t * TILE + TILE)
            p = jnp.exp(dot(k_s[h, ts, :], q, 1, 1) - lse)
            dp = dot(v_s[h, ts, :], a, 1, 1)
            p_s[ts, :] = p
            dp_s[ts, :] = dp
            delta = delta + jnp.sum((p * dp).reshape(TILE // 8, 8, ROWS), axis=0)
        delta = jnp.sum(delta, axis=0, keepdims=True)
        att = jnp.zeros((HD, ROWS), F32)
        dq = jnp.zeros((HD, ROWS), F32)
        for t in range(SEQ // TILE):
            ts = slice(t * TILE, t * TILE + TILE)
            p = p_s[ts, :]
            pb = p.astype(BF)
            ds = (p * (dp_s[ts, :] - delta)).astype(BF)
            att += dot(vt_s[h, t], pb, 1, 0)
            dq += dot(kt_s[h, t], ds, 1, 0)
            dk_s[:, ts] += dot(qt, ds, 1, 1)
            dv_s[:, ts] += dot(at_, pb, 1, 1)
        p_buf[c, base:base + HD, :] = att.astype(BF)
        p_buf[c, base + HD:base + 2 * HD, :] = (SCALE * dq).astype(BF)

    def sent(kind, c):
        rows = slice((0, 128, 256, 384)[kind], (128, 256, 384, 512)[kind])
        return remote(
            p_buf.at[c, rows], b_buf.at[d, rows], ps.at[kind, c], pr.at[kind, d], at(c, r)
        )

    def came(kind, c):
        rows = slice((0, 128, 256, 384)[kind], (128, 256, 384, 512)[kind])
        return remote(
            p_buf.at[c, rows], b_buf.at[c, rows], ps.at[kind, c], pr.at[kind, c], at(c, r)
        )

    def totals(base, kind):
        for c in range(ND):
            cols = slice(c * ROWS, c * ROWS + ROWS)
            p_buf[c, base:base + HD, :] = dk_s[:, cols].astype(BF)
            p_buf[c, base + HD:base + 2 * HD, :] = dv_s[:, cols].astype(BF)
        for s in range(1, ND):
            sent(kind, (d + s) % ND).start()

    def attend_shared(i, _):
        c = 4 * par + i
        attend(1, c, 384)
        pl.when(c != d)(lambda: sent(3, c).start())
        return 0

    def attend_own(c, _):
        attend(0, c, 0)
        pl.when(c != d)(lambda: sent(0, c).start())
        return 0

    dk_s[...] = jnp.zeros_like(dk_s)
    dv_s[...] = jnp.zeros_like(dv_s)
    lax.fori_loop(0, 4, attend_shared, 0)
    totals(256, 2)
    wait(u2)
    start(u4)
    dk_s[...] = jnp.zeros_like(dk_s)
    dv_s[...] = jnp.zeros_like(dv_s)
    lax.fori_loop(0, 8, attend_own, 0)
    totals(128, 1)
    local = pltpu.make_async_copy(p_buf.at[d], b_buf.at[d], loc.at[2])
    local.start()
    wait(u3)
    wait(u4)
    own_u.wait()

    gt_s[...] = jnp.zeros_like(gt_s)
    ga_s[...] = jnp.zeros_like(ga_s)

    def grads(c, _):
        n, u = n_all[c], u_all[c]
        gt_s[0:320] += dot(p_buf[c, 64:384], n, 1, 0)
        gt_s[320:384] += dot(p_buf[c, 448:512], n, 1, 0)
        ga_s[0:64] += dot(p_buf[c, 0:64], u, 1, 0)
        ga_s[64:128] += dot(p_buf[c, 384:448], u, 1, 0)
        return 0

    lax.fori_loop(0, ND, grads, 0)
    gt = gt_s[...].astype(BF)
    ga = ga_s[...].astype(BF)

    def order(b, _):
        R = lax.broadcasted_iota(jnp.int32, (256, E), 0) + b * 256
        F = lax.broadcasted_iota(jnp.int32, (256, E), 1)
        i = R % 8
        g = moved(hot((F == 6 * (16 * ((R // 8) % 8) + R // 64) + i) & (i < 6)), gt, 1, 1)
        for s in range(4):
            rs[4 * b + s, 0:64, :] = g[64 * s:64 * s + 64]
        return 0

    lax.fori_loop(0, 4, order, 0)
    R = lax.broadcasted_iota(jnp.int32, (256, 128), 0)
    C = lax.broadcasted_iota(jnp.int32, (256, 128), 1)
    i = R % 8
    feature = jnp.where(C < 64, C + 128 * par, C)
    g = moved(hot((feature == 96 * ((R // 8) % 2) + 6 * (R // 16) + i) & (i < 6)), ga, 1, 0)
    for s in range(NR):
        rs[s, 64:80, :] = g[16 * s:16 * s + 16, 0:384]
        rs[s, 80:96, :] = g[16 * s:16 * s + 16, 384:768]
    cc = [
        remote(rs.at[2 * g + 1 - core], bc.at[g], gs.at[g], gr.at[g], c_peer) for g in range(8)
    ]
    start(cc)

    wait(wc3)
    for g in range(8):
        s1 = wl[g // 4, g % 4].reshape(256, E)
        s2 = wr[g // 4, g % 4].reshape(256, 384)
        rows = slice(96 * g, 96 * g + 96)
        w_full[0, rows] = moved(hot_s[0], s1, 1, 0)
        w_full[1, rows] = moved(hot_s[1], s1, 1, 0)
        w_full[2, rows] = moved(hot_s[2], s1, 1, 0)
        w_full[2, rows, 0:384] += moved(hot_s[3], s2, 1, 0)
        w_full[2, rows, 384:768] += moved(hot_s[4], s2, 1, 0)

    for g in range(8):
        cc[g].wait()
        acc1[g] = (rs[2 * g + core].astype(F32) + bc[g].astype(F32)).astype(BF)
    cz = []
    for s in range(1, 4):
        to = (z + s) % 4
        for q in range(2):
            k = 8 + (s - 1) * 2 + q
            cz.append(remote(acc1.at[q * 4 + to], bz.at[s - 1, q], gs.at[k], gr.at[k], z_peers[s - 1]))
    start(cz)

    local.wait()
    for kind in range(3):
        for s in range(1, ND):
            came(kind, (d + s) % ND).wait_recv()
    for s in range(1, ND):
        c = (d + s) % ND
        pl.when(c % 2 == half)(came(3, c).wait_recv)
    for k in range(4):
        lo, hi = 2 * k, 2 * k + 1
        sh = 2 * k + half
        for m in range(4):
            t_s[m, 192 * k:192 * k + 64] = b_buf[lo, 64 * m:64 * m + 64]
            t_s[m, 192 * k + 128:192 * k + 192] = b_buf[hi, 64 * m:64 * m + 64]
        for m in range(2):
            t_s[m, 192 * k + 64:192 * k + 128] = b_buf[sh, 384 + 64 * m:448 + 64 * m]
            rows = slice(256 + 64 * m, 320 + 64 * m)
            t_s[2 + m, 192 * k + 64:192 * k + 128] = (
                b_buf[lo, rows].astype(F32) + b_buf[hi, rows].astype(F32)
            ).astype(BF)

    wait(cz)
    for q in range(2):
        acc2[q] = (
            acc1[q * 4 + z].astype(F32)
            + bz[0, q].astype(F32)
            + bz[1, q].astype(F32)
            + bz[2, q].astype(F32)
        ).astype(BF)
    cx = remote(acc2.at[1 - xl], bx, gs.at[14], gr.at[14], x_peers[1])
    cx.start()
    out_ref[...] = (x_ref[...].astype(F32) + dot(t_s[0].T, w_full[3], 1, 0)).astype(BF)
    cx.wait()
    acc3[...] = acc2[xl].astype(F32) + bx[...].astype(F32)
    last = []
    for s in range(1, ND):
        to = (d + s) % ND
        rows = pl.ds(pl.multiple_of(to * 8, 8), 8)
        last.append(remote(acc3.at[rows], finq.at[d], gs.at[14 + s], gr.at[14 + s], depth_peers[s - 1]))
    partner = at(d + 1 - 2 * par, r)
    for k in range(2):
        rows = pl.ds(pl.multiple_of(64 + k * 16 + (1 - par) * 8, 8), 8)
        last.append(remote(acc3.at[rows], fino.at[k], gs.at[22 + k], gr.at[22 + k], partner))
    start(last)
    finq[d] = acc3[pl.ds(pl.multiple_of(d * 8, 8), 8), :]

    dn = dot(t_s[1].T, w_full[0], 1, 1)
    dn += dot(t_s[2].T, w_full[1], 1, 1)
    dn += dot(t_s[3].T, w_full[2], 1, 1)
    x = x_ref[...].astype(F32)
    centered = x - jnp.mean(x, axis=-1, keepdims=True)
    inverse = lax.rsqrt(jnp.mean(centered * centered, axis=-1, keepdims=True) + 1e-05)
    unit = centered * inverse
    du = dn * gain_ref[...]
    al_ref[...] = (
        u_ref[...].astype(F32)
        + inverse
        * (du - jnp.mean(du, axis=-1, keepdims=True) - unit * jnp.mean(du * unit, axis=-1, keepdims=True))
    ).astype(BF)

    wait(last)
    places = ((0, 320), (64, 192), (128, 256))
    dgain = jnp.zeros((6, 1), F32)
    for m, (g_ref, w_ref) in enumerate(((gq_ref, wq_ref), (gk_ref, wk_ref), (gv_ref, wv_ref))):
        own, sh = places[m]
        parts = []
        for k in range(4):
            parts.append(finq[2 * k, 0:6, own:own + 64])
            parts.append(finq[2 * k, 0:6, sh:sh + 64] + finq[2 * k + 1, 0:6, sh:sh + 64])
            parts.append(finq[2 * k + 1, 0:6, own:own + 64])
        g = jnp.concatenate(parts, axis=1)
        g_ref[...] = g
        dgain = dgain + jnp.sum(g * w_ref[...].astype(F32), axis=1, keepdims=True)
    for k in range(2):
        rows = pl.ds(pl.multiple_of(64 + k * 16 + par * 8, 8), 8)
        go_ref[:, k * 384:k * 384 + 384] = (acc3[rows, :] + fino[k])[0:6]
    F = lax.broadcasted_iota(jnp.int32, (6, E), 1)
    I = lax.broadcasted_iota(jnp.int32, (6, E), 0)
    own_gain = jnp.sum(
        jnp.where(F == 6 * (NR * d + r) + I, gain_ref[...], 0.0), axis=1, keepdims=True
    )
    dg_ref[...] = jnp.broadcast_to(dgain / own_gain, (6, 128))

    for kind in range(3):
        for s in range(1, ND):
            sent(kind, (d + s) % ND).wait_send()
    for i in range(4):
        c = 4 * par + i
        pl.when(c != d)(sent(3, c).wait_send)


def fused(x, u, gain, wq, wk, wv, we):
    vm = pl.BlockSpec(memory_space=pltpu.VMEM)
    dma = lambda *shape: pltpu.SemaphoreType.DMA(shape)
    grad = jax.ShapeDtypeStruct((6, E), F32)
    return pl.pallas_call(
        kernel,
        out_shape=(
            jax.ShapeDtypeStruct((ROWS, E), BF),
            jax.ShapeDtypeStruct((ROWS, E), BF),
            grad, grad, grad, grad,
            jax.ShapeDtypeStruct((6, 128), F32),
        ),
        in_specs=[vm] * 7,
        out_specs=(vm,) * 7,
        scratch_shapes=[
            pltpu.VMEM((ND, ROWS, E), BF),
            pltpu.VMEM((ND, ROWS, E), BF),
            pltpu.VMEM((2, 4, 2, 8, 16, E), BF),
            pltpu.VMEM((2, 4, 2, 8, 16, 384), BF),
            pltpu.VMEM((2, 4, 2, 8, 16, 256), BF),
            pltpu.VMEM((4, E, E), BF),
            pltpu.VMEM((7, 96, 256), BF),
            pltpu.VMEM((3, E, 128), BF),
            pltpu.VMEM((2, SEQ, HD), BF),
            pltpu.VMEM((2, SEQ, HD), BF),
            pltpu.VMEM((2, SEQ, HD), BF),
            pltpu.VMEM((2, SEQ, HD), BF),
            pltpu.VMEM((2, ND, HD, ROWS), BF),
            pltpu.VMEM((2, ND, HD, ROWS), BF),
            pltpu.VMEM((ND, ROWS, 128), BF),
            pltpu.VMEM((ND, ROWS, 128), BF),
            pltpu.VMEM((2, ND, 1, ROWS), F32),
            pltpu.VMEM((SEQ, ROWS), F32),
            pltpu.VMEM((SEQ, ROWS), F32),
            pltpu.VMEM((HD, SEQ), F32),
            pltpu.VMEM((HD, SEQ), F32),
            pltpu.VMEM((ND, 512, ROWS), BF),
            pltpu.VMEM((ND, 512, ROWS), BF),
            pltpu.VMEM((384, E), F32),
            pltpu.VMEM((128, E), F32),
            pltpu.VMEM((NR, 96, 384), BF),
            pltpu.VMEM((8, 96, 384), BF),
            pltpu.VMEM((8, 96, 384), BF),
            pltpu.VMEM((3, 2, 96, 384), BF),
            pltpu.VMEM((2, 96, 384), BF),
            pltpu.VMEM((96, 384), BF),
            pltpu.VMEM((96, 384), F32),
            pltpu.VMEM((ND, 8, 384), F32),
            pltpu.VMEM((2, 8, 384), F32),
            pltpu.VMEM((4, E, ROWS), BF),
            dma(9), dma(9), dma(9), dma(9), dma(33), dma(33), dma(7), dma(7),
            dma(4, ND), dma(4, ND), dma(24), dma(24), dma(3),
        ],
        compiler_params=pltpu.CompilerParams(
            collective_id=1, has_side_effects=True, vmem_limit_bytes=VMEM_LIMIT
        ),
        name="fused",
    )(x, u, gain, wq, wk, wv, we)


def body(x, gain, wq, wk, wv, we, u):
    out, al, gq, gk, gv, go, dg = fused(
        x.reshape(ROWS, E), u.reshape(ROWS, E), gain.reshape(1, E), wq, wk, wv, we
    )
    return out.reshape(ROWS, 1, E), al.reshape(ROWS, 1, E), gq, gk, gv, go, dg[:, 0]


def solution(mesh):
    rows = P("depth", "res", None)
    shard = P(("depth", "res"), None)
    return jax.shard_map(
        body,
        mesh=mesh,
        in_specs=(rows, P(), shard, shard, shard, shard, rows),
        out_specs=(rows, rows, shard, shard, shard, shard, P(("depth", "res"))),
        check_vma=False,
    )
```

```python
import jax
import jax.numpy as jnp
from jax import lax
from jax.experimental import pallas as pl
from jax.experimental.pallas import tpu as pltpu
from jax.sharding import PartitionSpec as P

HD = 64
E = 768
ND = 8
NR = 16
ROWS = 256
SEQ = ND * ROWS
TILE = 256
SCALE = HD ** (-0.5)
MESH = pl.DeviceIdType.MESH
BF = jnp.bfloat16
F32 = jnp.float32
VMEM_LIMIT = 58 * 1024 * 1024


def place():
    d = lax.axis_index("depth")
    r = lax.axis_index("res")
    return d, r, d // 4, d % 4, r // 8, (r // 2) % 4, r % 2


def at(d, r):
    return {"depth": d, "res": r}


def barrier(peers):
    sem = pltpu.get_barrier_semaphore()
    for peer in peers:
        pl.semaphore_signal(sem, inc=1, device_id=peer, device_id_type=MESH)
    pl.semaphore_wait(sem, len(peers))


def remote(src, dst, send, recv, peer):
    return pltpu.make_async_remote_copy(
        src_ref=src, dst_ref=dst, send_sem=send, recv_sem=recv, device_id=peer, device_id_type=MESH
    )


def start(copies):
    for c in copies:
        c.start()


def wait(copies):
    for c in copies:
        c.wait()


def dot(a, b, ca, cb):
    return lax.dot_general(a, b, (((ca,), (cb,)), ((), ())), preferred_element_type=F32)


def hot(mask):
    return jnp.where(mask, 1.0, 0.0).astype(BF)


def moved(a, b, ca, cb):
    return dot(a, b, ca, cb).astype(BF)


SPLIT = 64
KINDS = ((0, 64), (64, 128), (128, 192), (192, 320), (320, 448), (448, 512))


def ring(full, d, xh, y, r, ss, rs):
    e = (d + 4) % ND
    across, up, down = at(e, r), at(xh * 4 + (y + 1) % 4, r), at(xh * 4 + (y + 3) % 4, r)
    lo, hi, far = xh * 4 + (y + 3) % 4, xh * 4 + (y + 1) % 4, xh * 4 + (y + 2) % 4
    mid = SPLIT + 96

    def send(k, peer, block, rows):
        return remote(full.at[block, rows], full.at[block, rows], ss.at[k], rs.at[k], peer)

    whole = slice(0, ROWS)
    c0 = send(0, across, d, whole)
    near = (send(1, up, d, whole), send(2, down, d, whole))
    near2 = (send(3, up, e, slice(SPLIT, ROWS)), send(4, down, e, slice(SPLIT, ROWS)))
    on = (send(5, up, lo, slice(0, 128)), send(6, down, hi, slice(128, ROWS)))
    cross = (send(7, across, lo, slice(0, SPLIT)), send(8, across, hi, slice(0, SPLIT)))
    cross2 = (send(9, across, far, slice(0, SPLIT)),)
    lo2, hi2 = (lo + 4) % ND, (hi + 4) % ND
    on2 = (send(10, up, lo2, slice(SPLIT, mid)), send(11, down, hi2, slice(mid, ROWS)))
    return c0, near, near2, on, cross, cross2, on2


def kernel(
    x_hbm, u_hbm, gain_ref, wq_ref, wk_ref, wv_ref, we_ref,
    out_hbm, al_hbm, gq_ref, gk_ref, gv_ref, go_ref, dg_ref,
    x_ref, u_ref, out_ref, al_ref, n_all, wl, wr, wc, w_full, hot_s, sel_s, perm_g, perm_o,
    q_s, k_s, v_s, a_s, kt_s, vt_s, a_out, a_in, lse_s, p_s, dp_s, dk_s, dv_s,
    p_buf, b_buf, gt_s, rs, bc, acc1, bz, acc2, bx, acc3, finq, t_s,
    ro, boc, oc, boz, ox, box, oy, boy,
    ns, nr, ws, wrs, as_, ar, ps, pr, gs, gr, os_, or_, loc,
):
    d, r, xh, y, xl, z, core = place()
    par, j, half = d % 2, d // 2, d // 4
    zc = z * 2 + core
    depth_peers = [at((d + s) % ND, r) for s in range(1, ND)]
    y_peers = [at(xh * 4 + (y + s) % 4, r) for s in range(1, 4)]
    x_peers = [at((1 - xh) * 4 + y, r), at(d, (1 - xl) * 8 + zc), at((1 - xh) * 4 + y, (1 - xl) * 8 + zc)]
    z_peers = [at(d, xl * 8 + ((z + s) % 4) * 2 + core) for s in range(1, 4)]
    z_from = [((z + 4 - s) % 4) * 2 + core for s in range(1, 4)]
    c_peer = at(d, xl * 8 + z * 2 + 1 - core)
    x_in = pltpu.make_async_copy(x_hbm, x_ref, loc.at[3])
    u_in = pltpu.make_async_copy(u_hbm, u_ref, loc.at[4])
    x_in.start()
    u_in.start()
    barrier(depth_peers + x_peers[1:] + z_peers + [c_peer])

    top = jnp.concatenate(
        [wq_ref[...].astype(F32), wk_ref[...].astype(F32), wv_ref[0:4].astype(F32)], axis=0
    )
    rest = jnp.concatenate([wv_ref[4:6].astype(F32), we_ref[...].astype(F32)], axis=0)
    rest = jnp.concatenate([rest[:, 0:384], rest[:, 384:768]], axis=0)
    wl[xh, y, xl, zc] = top.astype(BF)
    wr[xh, y, xl, zc] = rest.astype(BF)
    wy = []
    for s in range(3):
        for k, w in enumerate((wl, wr)):
            one = w.at[xh, y, xl, zc]
            wy.append(remote(one, one, ws.at[2 * s + k], wrs.at[2 * s + k], y_peers[s]))
    start(wy)

    x_in.wait()
    gain = gain_ref[...].reshape(1, E)
    x = x_ref[...].astype(F32)
    centered = x - jnp.mean(x, axis=-1, keepdims=True)
    inverse = lax.rsqrt(jnp.mean(centered * centered, axis=-1, keepdims=True) + 1e-05)
    n_all[d] = (centered * inverse * gain).astype(BF)
    n0, n_near, n_near2, n_on, n_cross, n_cross2, n_on2 = ring(n_all, d, xh, y, r, ns, nr)
    n0.start()

    window = pl.multiple_of(128 * ((3 * j) // 2), 128)
    offset = 192 * j - 128 * ((3 * j) // 2)
    other = pl.multiple_of(128 * ((3 * (2 * (1 - xh) + y // 2)) // 2), 128)
    wait(wy)
    start(n_near)
    windows = (other, window, other)
    wx = []
    for s in range(3):
        mine = wl.at[xh, :, xl, zc, :, pl.ds(windows[s], 256)]
        wx.append(remote(mine, wc.at[xh, :, xl, zc], ws.at[6 + 2 * s], wrs.at[6 + 2 * s], x_peers[s]))
        slab = wr.at[xh, :, xl, zc]
        wx.append(remote(slab, slab, ws.at[7 + 2 * s], wrs.at[7 + 2 * s], x_peers[s]))
    start(wx)
    own_w = pltpu.make_async_copy(
        wl.at[xh, :, xl, zc, :, pl.ds(window, 256)], wc.at[xh, :, xl, zc], loc.at[1]
    )
    own_w.start()
    R = lax.broadcasted_iota(jnp.int32, (96, 256), 0)
    K = lax.broadcasted_iota(jnp.int32, (96, 256), 1)
    o16, i6 = 16 * (R // 6), R % 6
    hot_s[0] = hot(K == o16 + i6)
    hot_s[1] = hot(K == o16 + 6 + i6)
    hot_s[2] = hot((K == o16 + 12 + i6) & (i6 < 4))
    hot_s[3] = hot((K == o16 + i6 - 4) & (i6 >= 4))
    hot_s[4] = hot((K == o16 + 8 + i6 - 4) & (i6 >= 4))
    hot_s[5] = hot(K == o16 + 2 + i6)
    hot_s[6] = hot(K == o16 + 10 + i6)
    K2 = lax.broadcasted_iota(jnp.int32, (256, 128), 0)
    C2 = lax.broadcasted_iota(jnp.int32, (256, 128), 1)
    pick = hot(K2 == jnp.where(C2 < 64, offset + 128 * par + C2, offset + C2))
    n0.wait()
    start(n_near2)
    wait(wx)
    own_w.wait()

    slab = wc.at[:, :, :, zc]
    wz1 = [remote(slab, slab, ws.at[12 + s], wrs.at[12 + s], z_peers[s]) for s in range(3)]
    start(wz1)
    wc1 = [remote(slab, slab, ws.at[15], wrs.at[15], c_peer)]
    start(wc1)
    slab = wr.at[:, :, :, zc]
    wz2 = [remote(slab, slab, ws.at[19 + s], wrs.at[19 + s], z_peers[s]) for s in range(3)]
    start(wz2)
    wc2 = [remote(slab, slab, ws.at[22], wrs.at[22], c_peer)]
    start(wc2)
    wait(n_near)
    start(n_on)
    start(n_cross)
    slab = wl.at[xh, :, xl, zc]
    wx2 = [remote(slab, slab, ws.at[33 + s], wrs.at[33 + s], x_peers[s]) for s in range(3)]
    start(wx2)
    p_buf[:, 448:512, :] = jnp.zeros((ND, 64, ROWS), BF)

    def orders(b, _):
        R = lax.broadcasted_iota(jnp.int32, (64, E), 0)
        F = lax.broadcasted_iota(jnp.int32, (64, E), 1)
        i = R % 8
        owner = 16 * ((R // 8) % 8) + 2 * (b % 8) + b // 8
        perm_g[b // 8, b % 8] = hot((F == 6 * owner + i) & (i < 6))
        return 0

    lax.fori_loop(0, NR, orders, 0)

    def orders_o(b, _):
        R = lax.broadcasted_iota(jnp.int32, (96, E), 0)
        F = lax.broadcasted_iota(jnp.int32, (96, E), 1)
        q = R // 24
        owner = (((q // 2) * 4 + (R // 6) % 4) * 2 + q % 2) * 8 + (b % 4) * 2 + b // 4
        perm_o[b] = hot(F == 6 * owner + R % 6)
        return 0

    lax.fori_loop(0, 8, orders_o, 0)

    for s in range(3):
        wz1[s].wait()
        there = wc.at[:, :, :, z_from[s]]
        c = remote(there, there, ws.at[16 + s], wrs.at[16 + s], c_peer)
        c.start()
        wc1.append(c)
    wait(n_near2)
    start(n_on2)
    wait(n_on)
    start(n_cross2)
    wait(wc1)

    for g in range(8):
        s1 = moved(wc[g // 4, g % 4].reshape(256, 256), pick, 1, 0)
        rows = slice(96 * g, 96 * g + 96)
        for m in range(3):
            sel_s[rows, 128 * m:128 * m + 128] = moved(hot_s[m], s1, 1, 0)

    for s in range(3):
        wz2[s].wait()
        there = wr.at[:, :, :, z_from[s]]
        c = remote(there, there, ws.at[23 + s], wrs.at[23 + s], c_peer)
        c.start()
        wc2.append(c)
    wait(wx2)
    slab = wl.at[:, :, :, zc]
    wz3 = [remote(slab, slab, ws.at[26 + s], wrs.at[26 + s], z_peers[s]) for s in range(3)]
    start(wz3)
    wc3 = [remote(slab, slab, ws.at[29], wrs.at[29], c_peer)]
    start(wc3)
    wait(wc2)
    u_in.wait()
    for g in range(8):
        s2 = wr[g // 4, g % 4].reshape(256, 384)
        rows = slice(96 * g, 96 * g + 96)
        w_full[3, rows, 0:384] = moved(hot_s[5], s2, 1, 0)
        w_full[3, rows, 384:768] = moved(hot_s[6], s2, 1, 0)
    a = dot(u_ref[...], w_full[3], 1, 1).astype(BF)
    for t in range(ND):
        own, sh = 192 * (t // 2) + 128 * (t % 2), 192 * (t // 2) + 64
        a_out[t] = jnp.concatenate([a[:, own:own + HD], a[:, sh:sh + HD]], axis=1)
    ca = []
    for s in range(1, ND):
        c = remote(a_out.at[(d + s) % ND], a_in.at[d], as_.at[s - 1], ar.at[s - 1], depth_peers[s - 1])
        c.start()
        ca.append(c)
    a_in[d] = a_out[d]

    inner = pl.multiple_of(128 * ((3 * j) // 2) - 384 * half, 128)
    for g in range(8):
        s2 = moved(wr[g // 4, g % 4, :, :, :, pl.ds(inner, 256)].reshape(256, 256), pick, 1, 0)
        late = jnp.where(half == 0, hot_s[3], hot_s[4])
        rows = slice(96 * g, 96 * g + 96)
        sel_s[rows, 256:384] = sel_s[rows, 256:384] + moved(late, s2, 1, 0)

    def project(i, group):
        c = group * 4 + (y + i) % 4
        rows = pl.ds(pl.multiple_of(c * ROWS, ROWS), ROWS)
        qkv = dot(n_all[c], sel_s[...], 1, 0)
        q = (SCALE * qkv[:, 0:128]).astype(BF)
        k = qkv[:, 128:256].astype(BF)
        v = qkv[:, 256:384].astype(BF)
        kt = k.T
        vt = v.T
        for h in range(2):
            q_s[h, rows, :] = q[:, h * HD:h * HD + HD]
            k_s[h, rows, :] = k[:, h * HD:h * HD + HD]
            v_s[h, rows, :] = v[:, h * HD:h * HD + HD]
            kt_s[h, c] = kt[h * HD:h * HD + HD]
            vt_s[h, c] = vt[h * HD:h * HD + HD]
        return group

    lax.fori_loop(0, 4, project, xh)
    wait(n_on2)
    wait(n_cross)
    wait(n_cross2)
    lax.fori_loop(0, 4, project, 1 - xh)

    def sent(kind, c):
        rows = slice(*KINDS[kind])
        return remote(
            p_buf.at[c, rows], b_buf.at[d, rows], ps.at[kind, c], pr.at[kind, d], at(c, r)
        )

    def came(kind, c):
        rows = slice(*KINDS[kind])
        return remote(
            p_buf.at[c, rows], b_buf.at[c, rows], ps.at[kind, c], pr.at[kind, c], at(c, r)
        )

    def forward(h, c):
        q = q_s[h, pl.ds(pl.multiple_of(c * ROWS, ROWS), ROWS), :]
        m = jnp.full((8, ROWS), -jnp.inf, F32)
        for t in range(SEQ // TILE):
            ts = slice(t * TILE, t * TILE + TILE)
            s = dot(k_s[h, ts, :], q, 1, 1)
            p_s[ts, :] = s
            m = jnp.maximum(m, jnp.max(s.reshape(TILE // 8, 8, ROWS), axis=0))
        m = jnp.max(m, axis=0, keepdims=True)
        l = jnp.zeros((8, ROWS), F32)
        att = jnp.zeros((HD, ROWS), F32)
        for t in range(SEQ // TILE):
            e = jnp.exp(p_s[t * TILE:t * TILE + TILE, :] - m)
            l = l + jnp.sum(e.reshape(TILE // 8, 8, ROWS), axis=0)
            att += dot(vt_s[h, t], e.astype(BF), 1, 0)
        l = jnp.sum(l, axis=0, keepdims=True)
        p_buf[c, h * HD:h * HD + HD, :] = (att * (1.0 / l)).astype(BF)
        lse_s[h, c] = m + jnp.log(l)
        pl.when(c != d)(lambda: sent(h, c).start())

    def forward_shared(i, _):
        forward(1, 4 * par + i)
        return 0

    def forward_own(i, _):
        forward(0, i)
        return 0

    lax.fori_loop(0, 4, forward_shared, 0)
    lax.fori_loop(0, 8, forward_own, 0)
    local = pltpu.make_async_copy(p_buf.at[d, 0:128], b_buf.at[d, 0:128], loc.at[0])
    local.start()
    wait(ca)

    def spread(c, _):
        rows = pl.ds(pl.multiple_of(c * ROWS, ROWS), ROWS)
        got = a_in[c]
        a_s[0, rows, :] = got[:, 0:HD]
        a_s[1, rows, :] = got[:, HD:2 * HD]
        return 0

    lax.fori_loop(0, ND, spread, 0)
    for s in range(3):
        wz3[s].wait()
        there = wl.at[:, :, :, z_from[s]]
        c = remote(there, there, ws.at[30 + s], wrs.at[30 + s], c_peer)
        c.start()
        wc3.append(c)

    def attend(h, c, base):
        rows = pl.ds(pl.multiple_of(c * ROWS, ROWS), ROWS)
        q = q_s[h, rows, :]
        a = a_s[h, rows, :]
        qt, at_ = q.T, a.T
        lse = lse_s[h, c]
        delta = jnp.zeros((8, ROWS), F32)
        for t in range(SEQ // TILE):
            ts = slice(t * TILE, t * TILE + TILE)
            p = jnp.exp(dot(k_s[h, ts, :], q, 1, 1) - lse)
            dp = dot(v_s[h, ts, :], a, 1, 1)
            p_s[ts, :] = p
            dp_s[ts, :] = dp
            delta = delta + jnp.sum((p * dp).reshape(TILE // 8, 8, ROWS), axis=0)
        delta = jnp.sum(delta, axis=0, keepdims=True)
        dq = jnp.zeros((HD, ROWS), F32)
        for t in range(SEQ // TILE):
            ts = slice(t * TILE, t * TILE + TILE)
            p = p_s[ts, :]
            pb = p.astype(BF)
            ds = (p * (dp_s[ts, :] - delta)).astype(BF)
            dq += dot(kt_s[h, t], ds, 1, 0)
            dk_s[:, ts] += dot(qt, ds, 1, 1)
            dv_s[:, ts] += dot(at_, pb, 1, 1)
        p_buf[c, base:base + HD, :] = (SCALE * dq).astype(BF)

    def totals(base, kind):
        for c in range(ND):
            cols = slice(c * ROWS, c * ROWS + ROWS)
            p_buf[c, base:base + HD, :] = dk_s[:, cols].astype(BF)
            p_buf[c, base + HD:base + 2 * HD, :] = dv_s[:, cols].astype(BF)
        for s in range(1, ND):
            sent(kind, (d + s) % ND).start()

    def attend_shared(i, _):
        c = 4 * par + i
        attend(1, c, 448)
        pl.when(c != d)(lambda: sent(5, c).start())
        return 0

    def attend_own(c, _):
        attend(0, c, 128)
        pl.when(c != d)(lambda: sent(2, c).start())
        return 0

    def grads(h):
        rows = slice(128, 320) if h == 0 else slice(320, 512)
        for t in range(3):
            cols = slice(256 * t, 256 * t + 256)
            total = dot(p_buf[0, rows], n_all[0, :, cols], 1, 0)
            for c in range(1, ND):
                total += dot(p_buf[c, rows], n_all[c, :, cols], 1, 0)
            gt_s[:, cols] = total.astype(BF)
        for b in range(2):
            rs[h, b] = moved(perm_g[b].reshape(512, E), gt_s[...], 1, 1).reshape(8, 64, 192)

    def sum_cores(h, copies):
        for g in range(8):
            copies[g].wait()
            acc1[h, g] = (rs[h, core, g].astype(F32) + bc[h, g].astype(F32)).astype(BF)
        out = []
        for s in range(1, 4):
            for q in range(2):
                k = 8 + (s - 1) * 2 + q
                to = acc1.at[h, q * 4 + (z + s) % 4]
                out.append(remote(to, bz.at[h, s - 1, q], gs.at[h, k], gr.at[h, k], z_peers[s - 1]))
        start(out)
        return out

    def sum_z(h, copies):
        wait(copies)
        for q in range(2):
            acc2[h, q] = (
                acc1[h, q * 4 + z].astype(F32)
                + bz[h, 0, q].astype(F32)
                + bz[h, 1, q].astype(F32)
                + bz[h, 2, q].astype(F32)
            ).astype(BF)
        out = remote(acc2.at[h, 1 - xl], bx.at[h], gs.at[h, 14], gr.at[h, 14], x_peers[1])
        out.start()
        return out

    def sum_x(h, copy):
        copy.wait()
        acc3[h] = acc2[h, xl].astype(F32) + bx[h].astype(F32)
        out = []
        for s in range(1, ND):
            rows = pl.ds(pl.multiple_of(((d + s) % ND) * 8, 8), 8)
            out.append(
                remote(acc3.at[h, rows], finq.at[h, d], gs.at[h, 14 + s], gr.at[h, 14 + s], depth_peers[s - 1])
            )
        start(out)
        finq[h, d] = acc3[h, pl.ds(pl.multiple_of(d * 8, 8), 8), :]
        return out

    dk_s[...] = jnp.zeros_like(dk_s)
    dv_s[...] = jnp.zeros_like(dv_s)
    lax.fori_loop(0, 4, attend_shared, 0)
    totals(320, 4)
    grads(1)
    sc = [
        remote(rs.at[1, 1 - core, g], bc.at[1, g], gs.at[1, g], gr.at[1, g], c_peer) for g in range(8)
    ]
    start(sc)

    local.wait()
    for s in range(1, ND):
        c = (d + s) % ND
        came(0, c).wait_recv()
        pl.when(c % 2 == half)(came(1, c).wait_recv)
    for k in range(4):
        t_s[0, 192 * k:192 * k + 64] = b_buf[2 * k, 0:64]
        t_s[0, 192 * k + 64:192 * k + 128] = b_buf[2 * k + half, 64:128]
        t_s[0, 192 * k + 128:192 * k + 192] = b_buf[2 * k + 1, 0:64]
    out_ref[...] = (x_ref[...].astype(F32) + dot(t_s[0].T, w_full[3], 1, 0)).astype(BF)
    out_copy = pltpu.make_async_copy(out_ref, out_hbm, loc.at[5])
    out_copy.start()
    go = dot(t_s[0], u_ref[...], 1, 0).astype(BF)
    for k in range(8):
        ro[k // 4, k % 4] = moved(perm_o[k], go, 1, 0)
    oc_copies = [
        remote(ro.at[1 - core, k], boc.at[k], os_.at[k], or_.at[k], c_peer) for k in range(4)
    ]
    start(oc_copies)

    dk_s[...] = jnp.zeros_like(dk_s)
    dv_s[...] = jnp.zeros_like(dv_s)
    lax.fori_loop(0, 2, attend_own, 0)
    for k in range(4):
        oc_copies[k].wait()
        oc[k] = (ro[core, k].astype(F32) + boc[k].astype(F32)).astype(BF)
    oz_copies = [
        remote(oc.at[(z + s) % 4], boz.at[s - 1], os_.at[3 + s], or_.at[3 + s], z_peers[s - 1])
        for s in range(1, 4)
    ]
    start(oz_copies)
    sz = sum_cores(1, sc)
    lax.fori_loop(2, 5, attend_own, 0)
    wait(oz_copies)
    total = (
        oc[z].astype(F32) + boz[0].astype(F32) + boz[1].astype(F32) + boz[2].astype(F32)
    )
    gap = jnp.zeros((2, E), F32)
    for q in range(4):
        parts = []
        for t in range(4):
            parts += [total[24 * q + 6 * t:24 * q + 6 * t + 6], gap]
        ox[q] = jnp.concatenate(parts, axis=0).astype(BF)
    x_to = [(1 - xh) * 2 + xl, xh * 2 + 1 - xl, (1 - xh) * 2 + 1 - xl]
    ox_copies = [
        remote(ox.at[x_to[s]], box.at[s], os_.at[7 + s], or_.at[7 + s], x_peers[s]) for s in range(3)
    ]
    start(ox_copies)
    sx = sum_z(1, sz)
    lax.fori_loop(5, 7, attend_own, 0)
    wait(ox_copies)
    total = (
        ox[xh * 2 + xl].astype(F32) + box[0].astype(F32) + box[1].astype(F32) + box[2].astype(F32)
    )
    for t in range(4):
        oy[t] = total[8 * t:8 * t + 8]
    oy_copies = [
        remote(oy.at[(y + s) % 4], boy.at[s - 1], os_.at[9 + s], or_.at[9 + s], y_peers[s - 1])
        for s in range(1, 4)
    ]
    start(oy_copies)
    sd = sum_x(1, sx)
    lax.fori_loop(7, 8, attend_own, 0)
    totals(192, 3)
    local = pltpu.make_async_copy(p_buf.at[d, 128:512], b_buf.at[d, 128:512], loc.at[2])
    local.start()

    grads(0)
    cc = [
        remote(rs.at[0, 1 - core, g], bc.at[0, g], gs.at[0, g], gr.at[0, g], c_peer) for g in range(8)
    ]
    start(cc)

    wait(wc3)
    for g in range(8):
        s1 = wl[g // 4, g % 4].reshape(256, E)
        s2 = wr[g // 4, g % 4].reshape(256, 384)
        rows = slice(96 * g, 96 * g + 96)
        w_full[0, rows] = moved(hot_s[0], s1, 1, 0)
        w_full[1, rows] = moved(hot_s[1], s1, 1, 0)
        w_full[2, rows] = moved(hot_s[2], s1, 1, 0)
        w_full[2, rows, 0:384] += moved(hot_s[3], s2, 1, 0)
        w_full[2, rows, 384:768] += moved(hot_s[4], s2, 1, 0)

    cz = sum_cores(0, cc)

    local.wait()
    for s in range(1, ND):
        c = (d + s) % ND
        for kind in (2, 3, 4):
            came(kind, c).wait_recv()
        pl.when(c % 2 == half)(came(5, c).wait_recv)
    for k in range(4):
        lo, hi = 2 * k, 2 * k + 1
        for m in range(3):
            rows = slice(128 + 64 * m, 192 + 64 * m)
            t_s[1 + m, 192 * k:192 * k + 64] = b_buf[lo, rows]
            t_s[1 + m, 192 * k + 128:192 * k + 192] = b_buf[hi, rows]
        t_s[1, 192 * k + 64:192 * k + 128] = b_buf[lo + half, 448:512]
        for m in range(2):
            rows = slice(320 + 64 * m, 384 + 64 * m)
            t_s[2 + m, 192 * k + 64:192 * k + 128] = (
                b_buf[lo, rows].astype(F32) + b_buf[hi, rows].astype(F32)
            ).astype(BF)

    cx = sum_z(0, cz)
    dn = dot(t_s[1].T, w_full[0], 1, 1)
    dn += dot(t_s[2].T, w_full[1], 1, 1)
    dn += dot(t_s[3].T, w_full[2], 1, 1)
    last = sum_x(0, cx)
    x = x_ref[...].astype(F32)
    centered = x - jnp.mean(x, axis=-1, keepdims=True)
    inverse = lax.rsqrt(jnp.mean(centered * centered, axis=-1, keepdims=True) + 1e-05)
    unit = centered * inverse
    du = dn * gain
    al_ref[...] = (
        u_ref[...].astype(F32)
        + inverse
        * (du - jnp.mean(du, axis=-1, keepdims=True) - unit * jnp.mean(du * unit, axis=-1, keepdims=True))
    ).astype(BF)

    al_copy = pltpu.make_async_copy(al_ref, al_hbm, loc.at[6])
    al_copy.start()

    wait(sd)
    wait(last)
    places = ((0, 128), (64, 0), (128, 64))
    dgain = jnp.zeros((6, 1), F32)
    for m, (g_ref, w_ref) in enumerate(((gq_ref, wq_ref), (gk_ref, wk_ref), (gv_ref, wv_ref))):
        own, sh = places[m]
        parts = []
        for k in range(4):
            parts.append(finq[0, 2 * k, 0:6, own:own + 64])
            parts.append(finq[1, 2 * k, 0:6, sh:sh + 64] + finq[1, 2 * k + 1, 0:6, sh:sh + 64])
            parts.append(finq[0, 2 * k + 1, 0:6, own:own + 64])
        g = jnp.concatenate(parts, axis=1)
        g_ref[...] = g
        dgain = dgain + jnp.sum(g * w_ref[...].astype(F32), axis=1, keepdims=True)
    wait(oy_copies)
    go_ref[...] = (oy[y] + boy[0] + boy[1] + boy[2])[0:6]
    F = lax.broadcasted_iota(jnp.int32, (6, E), 1)
    I = lax.broadcasted_iota(jnp.int32, (6, E), 0)
    own_gain = jnp.sum(
        jnp.where(F == 6 * (NR * d + r) + I, gain, 0.0), axis=1, keepdims=True
    )
    dg_ref[0:6] = jnp.broadcast_to(dgain / own_gain, (6, 128))
    dg_ref[6:8] = jnp.zeros((2, 128), F32)

    out_copy.wait()
    al_copy.wait()
    for s in range(1, ND):
        for kind in (0, 2, 3, 4):
            sent(kind, (d + s) % ND).wait_send()
    for i in range(4):
        c = 4 * par + i
        for kind in (1, 5):
            pl.when(c != d)(sent(kind, c).wait_send)


def fused(x, u, gain, wq, wk, wv, we):
    vm = pl.BlockSpec(memory_space=pltpu.VMEM)
    hbm = pl.BlockSpec(memory_space=pl.ANY)
    dma = lambda *shape: pltpu.SemaphoreType.DMA(shape)
    grad = jax.ShapeDtypeStruct((6, E), F32)
    return pl.pallas_call(
        kernel,
        out_shape=(
            jax.ShapeDtypeStruct((ROWS, E), BF),
            jax.ShapeDtypeStruct((ROWS, E), BF),
            grad, grad, grad, grad,
            jax.ShapeDtypeStruct((8, 128), F32),
        ),
        in_specs=[hbm] * 2 + [vm] * 5,
        out_specs=(hbm, hbm) + (vm,) * 5,
        scratch_shapes=[
            pltpu.VMEM((ROWS, E), BF),
            pltpu.VMEM((ROWS, E), BF),
            pltpu.VMEM((ROWS, E), BF),
            pltpu.VMEM((ROWS, E), BF),
            pltpu.VMEM((ND, ROWS, E), BF),
            pltpu.VMEM((2, 4, 2, 8, 16, E), BF),
            pltpu.VMEM((2, 4, 2, 8, 16, 384), BF),
            pltpu.VMEM((2, 4, 2, 8, 16, 256), BF),
            pltpu.VMEM((4, E, E), BF),
            pltpu.VMEM((7, 96, 256), BF),
            pltpu.VMEM((E, 384), BF),
            pltpu.VMEM((2, 8, 64, E), BF),
            pltpu.VMEM((8, 96, E), BF),
            pltpu.VMEM((2, SEQ, HD), BF),
            pltpu.VMEM((2, SEQ, HD), BF),
            pltpu.VMEM((2, SEQ, HD), BF),
            pltpu.VMEM((2, SEQ, HD), BF),
            pltpu.VMEM((2, ND, HD, ROWS), BF),
            pltpu.VMEM((2, ND, HD, ROWS), BF),
            pltpu.VMEM((ND, ROWS, 128), BF),
            pltpu.VMEM((ND, ROWS, 128), BF),
            pltpu.VMEM((2, ND, 1, ROWS), F32),
            pltpu.VMEM((SEQ, ROWS), F32),
            pltpu.VMEM((SEQ, ROWS), F32),
            pltpu.VMEM((HD, SEQ), F32),
            pltpu.VMEM((HD, SEQ), F32),
            pltpu.VMEM((ND, 512, ROWS), BF),
            pltpu.VMEM((ND, 512, ROWS), BF),
            pltpu.VMEM((192, E), BF),
            pltpu.VMEM((2, 2, 8, 64, 192), BF),
            pltpu.VMEM((2, 8, 64, 192), BF),
            pltpu.VMEM((2, 8, 64, 192), BF),
            pltpu.VMEM((2, 3, 2, 64, 192), BF),
            pltpu.VMEM((2, 2, 64, 192), BF),
            pltpu.VMEM((2, 64, 192), BF),
            pltpu.VMEM((2, 64, 192), F32),
            pltpu.VMEM((2, ND, 8, 192), F32),
            pltpu.VMEM((4, E, ROWS), BF),
            pltpu.VMEM((2, 4, 96, E), BF),
            pltpu.VMEM((4, 96, E), BF),
            pltpu.VMEM((4, 96, E), BF),
            pltpu.VMEM((3, 96, E), BF),
            pltpu.VMEM((4, 32, E), BF),
            pltpu.VMEM((3, 32, E), BF),
            pltpu.VMEM((4, 8, E), F32),
            pltpu.VMEM((3, 8, E), F32),
            dma(12), dma(12), dma(36), dma(36), dma(7), dma(7),
            dma(6, ND), dma(6, ND), dma(2, 22), dma(2, 22), dma(13), dma(13), dma(7),
        ],
        compiler_params=pltpu.CompilerParams(
            collective_id=1, has_side_effects=True, vmem_limit_bytes=VMEM_LIMIT
        ),
        name="fused",
    )(x, u, gain, wq, wk, wv, we)


def finish_kernel(*refs):
    for k in range(6):
        refs[7 + k][...] = refs[k][...]
    refs[13][...] = refs[6][...].T[0, 0:6]


def finish(arrays):
    vm = pl.BlockSpec(memory_space=pltpu.VMEM)
    return pl.pallas_call(
        finish_kernel,
        out_shape=tuple(jax.ShapeDtypeStruct(a.shape, a.dtype) for a in arrays[:6])
        + (jax.ShapeDtypeStruct((6,), F32),),
        in_specs=[vm] * 7,
        out_specs=(vm,) * 7,
        name="finish",
    )(*arrays)


def body(x, gain, wq, wk, wv, we, u):
    out, al, gq, gk, gv, go, dg = finish(
        fused(x.reshape(ROWS, E), u.reshape(ROWS, E), gain, wq, wk, wv, we)
    )
    return out.reshape(ROWS, 1, E), al.reshape(ROWS, 1, E), gq, gk, gv, go, dg


def solution(mesh):
    rows = P("depth", "res", None)
    shard = P(("depth", "res"), None)
    return jax.shard_map(
        body,
        mesh=mesh,
        in_specs=(rows, P(), shard, shard, shard, shard, rows),
        out_specs=(rows, rows, shard, shard, shard, shard, P(("depth", "res"))),
        check_vma=False,
    )
```

```python
import jax
import jax.numpy as jnp
from jax import lax
from jax.experimental import pallas as pl
from jax.experimental.pallas import tpu as pltpu
from jax.sharding import PartitionSpec as P

HD = 64
E = 768
ND = 8
NR = 16
ROWS = 256
SEQ = ND * ROWS
TILE = 256
SCALE = HD ** (-0.5)
MESH = pl.DeviceIdType.MESH
BF = jnp.bfloat16
F32 = jnp.float32
VMEM_LIMIT = 58 * 1024 * 1024


def place():
    d = lax.axis_index("depth")
    r = lax.axis_index("res")
    return d, r, d // 4, d % 4, r // 8, (r // 2) % 4, r % 2


def at(d, r):
    return {"depth": d, "res": r}


def barrier(peers):
    sem = pltpu.get_barrier_semaphore()
    for peer in peers:
        pl.semaphore_signal(sem, inc=1, device_id=peer, device_id_type=MESH)
    pl.semaphore_wait(sem, len(peers))


def remote(src, dst, send, recv, peer):
    return pltpu.make_async_remote_copy(
        src_ref=src, dst_ref=dst, send_sem=send, recv_sem=recv, device_id=peer, device_id_type=MESH
    )


def start(copies):
    for c in copies:
        c.start()


def wait(copies):
    for c in copies:
        c.wait()


def dot(a, b, ca, cb):
    return lax.dot_general(a, b, (((ca,), (cb,)), ((), ())), preferred_element_type=F32)


def hot(mask):
    return jnp.where(mask, 1.0, 0.0).astype(BF)


def moved(a, b, ca, cb):
    return dot(a, b, ca, cb).astype(BF)


SPLIT = 64
KINDS = ((0, 64), (64, 128), (128, 192), (192, 320), (320, 448), (448, 512))


def ring(full, d, xh, y, r, ss, rs):
    e = (d + 4) % ND
    across, up, down = at(e, r), at(xh * 4 + (y + 1) % 4, r), at(xh * 4 + (y + 3) % 4, r)
    lo, hi, far = xh * 4 + (y + 3) % 4, xh * 4 + (y + 1) % 4, xh * 4 + (y + 2) % 4
    mid = SPLIT + 96

    def send(k, peer, block, rows):
        return remote(full.at[block, rows], full.at[block, rows], ss.at[k], rs.at[k], peer)

    whole = slice(0, ROWS)
    c0 = send(0, across, d, whole)
    near = (send(1, up, d, whole), send(2, down, d, whole))
    near2 = (send(3, up, e, slice(SPLIT, ROWS)), send(4, down, e, slice(SPLIT, ROWS)))
    on = (send(5, up, lo, slice(0, 128)), send(6, down, hi, slice(128, ROWS)))
    cross = (send(7, across, lo, slice(0, SPLIT)), send(8, across, hi, slice(0, SPLIT)))
    cross2 = (send(9, across, far, slice(0, SPLIT)),)
    lo2, hi2 = (lo + 4) % ND, (hi + 4) % ND
    on2 = (send(10, up, lo2, slice(SPLIT, mid)), send(11, down, hi2, slice(mid, ROWS)))
    return c0, near, near2, on, cross, cross2, on2


def kernel(
    x_hbm, u_hbm, gain_ref, wq_ref, wk_ref, wv_ref, we_ref,
    out_hbm, al_hbm, gq_ref, gk_ref, gv_ref, go_ref, dg_ref,
    x_ref, u_ref, out_ref, al_ref, n_all, wl, wr, wc, w_full, hot_s, sel_s, perm_g, perm_o,
    q_s, k_s, v_s, a_s, kt_s, vt_s, a_out, a_in, e_s, r_s, p_s, dp_s, dk_s, dv_s,
    p_buf, b_buf, gt_s, rs, bc, acc1, bz, acc3, finq, t_s,
    ro, boc, oc, boz, ox, box, oy, boy,
    ns, nr, ws, wrs, as_, ar, ps, pr, gs, gr, os_, or_, loc,
):
    d, r, xh, y, xl, z, core = place()
    par, j, half = d % 2, d // 2, d // 4
    zc = z * 2 + core
    depth_peers = [at((d + s) % ND, r) for s in range(1, ND)]
    y_peers = [at(xh * 4 + (y + s) % 4, r) for s in range(1, 4)]
    x_peers = [at((1 - xh) * 4 + y, r), at(d, (1 - xl) * 8 + zc), at((1 - xh) * 4 + y, (1 - xl) * 8 + zc)]
    z_peers = [at(d, xl * 8 + ((z + s) % 4) * 2 + core) for s in range(1, 4)]
    z_from = [((z + 4 - s) % 4) * 2 + core for s in range(1, 4)]
    c_peer = at(d, xl * 8 + z * 2 + 1 - core)
    g0 = xl * 4 + z
    g_peers = [at(d, 2 * ((g0 + s) % 8) + core) for s in range(1, 8)]
    x_in = pltpu.make_async_copy(x_hbm, x_ref, loc.at[3])
    u_in = pltpu.make_async_copy(u_hbm, u_ref, loc.at[4])
    x_in.start()
    u_in.start()
    barrier(depth_peers + x_peers[2:] + g_peers + [c_peer])

    top = jnp.concatenate(
        [wq_ref[...].astype(F32), wk_ref[...].astype(F32), wv_ref[0:4].astype(F32)], axis=0
    )
    rest = jnp.concatenate([wv_ref[4:6].astype(F32), we_ref[...].astype(F32)], axis=0)
    rest = jnp.concatenate([rest[:, 0:384], rest[:, 384:768]], axis=0)
    wl[xh, y, xl, zc] = top.astype(BF)
    wr[xh, y, xl, zc] = rest.astype(BF)
    wy = []
    for s in range(3):
        for k, w in enumerate((wl, wr)):
            one = w.at[xh, y, xl, zc]
            wy.append(remote(one, one, ws.at[2 * s + k], wrs.at[2 * s + k], y_peers[s]))
    start(wy)

    x_in.wait()
    gain = gain_ref[...].reshape(1, E)
    x = x_ref[...].astype(F32)
    centered = x - jnp.mean(x, axis=-1, keepdims=True)
    inverse = lax.rsqrt(jnp.mean(centered * centered, axis=-1, keepdims=True) + 1e-05)
    n_all[d] = (centered * inverse * gain).astype(BF)
    n0, n_near, n_near2, n_on, n_cross, n_cross2, n_on2 = ring(n_all, d, xh, y, r, ns, nr)
    n0.start()

    window = pl.multiple_of(128 * ((3 * j) // 2), 128)
    offset = 192 * j - 128 * ((3 * j) // 2)
    other = pl.multiple_of(128 * ((3 * (2 * (1 - xh) + y // 2)) // 2), 128)
    wait(wy)
    start(n_near)
    windows = (other, window, other)
    wx = []
    for s in range(3):
        mine = wl.at[xh, :, xl, zc, :, pl.ds(windows[s], 256)]
        wx.append(remote(mine, wc.at[xh, :, xl, zc], ws.at[6 + 2 * s], wrs.at[6 + 2 * s], x_peers[s]))
        slab = wr.at[xh, :, xl, zc]
        wx.append(remote(slab, slab, ws.at[7 + 2 * s], wrs.at[7 + 2 * s], x_peers[s]))
    start(wx)
    own_w = pltpu.make_async_copy(
        wl.at[xh, :, xl, zc, :, pl.ds(window, 256)], wc.at[xh, :, xl, zc], loc.at[1]
    )
    own_w.start()
    R = lax.broadcasted_iota(jnp.int32, (96, 256), 0)
    K = lax.broadcasted_iota(jnp.int32, (96, 256), 1)
    o16, i6 = 16 * (R // 6), R % 6
    hot_s[0] = hot(K == o16 + i6)
    hot_s[1] = hot(K == o16 + 6 + i6)
    hot_s[2] = hot((K == o16 + 12 + i6) & (i6 < 4))
    hot_s[3] = hot((K == o16 + i6 - 4) & (i6 >= 4))
    hot_s[4] = hot((K == o16 + 8 + i6 - 4) & (i6 >= 4))
    hot_s[5] = hot(K == o16 + 2 + i6)
    hot_s[6] = hot(K == o16 + 10 + i6)
    K2 = lax.broadcasted_iota(jnp.int32, (256, 128), 0)
    C2 = lax.broadcasted_iota(jnp.int32, (256, 128), 1)
    pick = hot(K2 == jnp.where(C2 < 64, offset + 128 * par + C2, offset + C2))
    n0.wait()
    start(n_near2)
    wait(wx)
    own_w.wait()

    slab = wc.at[:, :, :, zc]
    wz1 = [remote(slab, slab, ws.at[12 + s], wrs.at[12 + s], z_peers[s]) for s in range(3)]
    start(wz1)
    wc1 = [remote(slab, slab, ws.at[15], wrs.at[15], c_peer)]
    start(wc1)
    slab = wr.at[:, :, :, zc]
    wz2 = [remote(slab, slab, ws.at[19 + s], wrs.at[19 + s], z_peers[s]) for s in range(3)]
    start(wz2)
    wc2 = [remote(slab, slab, ws.at[22], wrs.at[22], c_peer)]
    start(wc2)
    wait(n_near)
    start(n_on)
    start(n_cross)
    slab = wl.at[xh, :, xl, zc]
    wx2 = [remote(slab, slab, ws.at[33 + s], wrs.at[33 + s], x_peers[s]) for s in range(3)]
    start(wx2)
    p_buf[:, 448:512, :] = jnp.zeros((ND, 64, ROWS), BF)

    def orders(b, _):
        R = lax.broadcasted_iota(jnp.int32, (64, E), 0)
        F = lax.broadcasted_iota(jnp.int32, (64, E), 1)
        i = R % 8
        owner = 16 * ((R // 8) % 8) + 2 * (b % 8) + b // 8
        perm_g[b // 8, b % 8] = hot((F == 6 * owner + i) & (i < 6))
        return 0

    lax.fori_loop(0, NR, orders, 0)

    def orders_o(b, _):
        R = lax.broadcasted_iota(jnp.int32, (96, E), 0)
        F = lax.broadcasted_iota(jnp.int32, (96, E), 1)
        q = R // 24
        owner = (((q // 2) * 4 + (R // 6) % 4) * 2 + q % 2) * 8 + (b % 4) * 2 + b // 4
        perm_o[b] = hot(F == 6 * owner + R % 6)
        return 0

    lax.fori_loop(0, 8, orders_o, 0)

    for s in range(3):
        wz1[s].wait()
        there = wc.at[:, :, :, z_from[s]]
        c = remote(there, there, ws.at[16 + s], wrs.at[16 + s], c_peer)
        c.start()
        wc1.append(c)
    wait(n_near2)
    start(n_on2)
    wait(n_on)
    start(n_cross2)
    wait(wc1)

    for g in range(8):
        s1 = moved(wc[g // 4, g % 4].reshape(256, 256), pick, 1, 0)
        rows = slice(96 * g, 96 * g + 96)
        for m in range(3):
            sel_s[rows, 128 * m:128 * m + 128] = moved(hot_s[m], s1, 1, 0)

    for s in range(3):
        wz2[s].wait()
        there = wr.at[:, :, :, z_from[s]]
        c = remote(there, there, ws.at[23 + s], wrs.at[23 + s], c_peer)
        c.start()
        wc2.append(c)
    wait(wx2)
    slab = wl.at[:, :, :, zc]
    wz3 = [remote(slab, slab, ws.at[26 + s], wrs.at[26 + s], z_peers[s]) for s in range(3)]
    start(wz3)
    wc3 = [remote(slab, slab, ws.at[29], wrs.at[29], c_peer)]
    start(wc3)
    wait(wc2)
    u_in.wait()
    for g in range(8):
        s2 = wr[g // 4, g % 4].reshape(256, 384)
        rows = slice(96 * g, 96 * g + 96)
        w_full[3, rows, 0:384] = moved(hot_s[5], s2, 1, 0)
        w_full[3, rows, 384:768] = moved(hot_s[6], s2, 1, 0)
    a = dot(u_ref[...], w_full[3], 1, 1).astype(BF)
    for t in range(ND):
        own, sh = 192 * (t // 2) + 128 * (t % 2), 192 * (t // 2) + 64
        a_out[t] = jnp.concatenate([a[:, own:own + HD], a[:, sh:sh + HD]], axis=1)
    ca = []
    for s in range(1, ND):
        c = remote(a_out.at[(d + s) % ND], a_in.at[d], as_.at[s - 1], ar.at[s - 1], depth_peers[s - 1])
        c.start()
        ca.append(c)
    a_in[d] = a_out[d]

    inner = pl.multiple_of(128 * ((3 * j) // 2) - 384 * half, 128)
    for g in range(8):
        s2 = moved(wr[g // 4, g % 4, :, :, :, pl.ds(inner, 256)].reshape(256, 256), pick, 1, 0)
        late = jnp.where(half == 0, hot_s[3], hot_s[4])
        rows = slice(96 * g, 96 * g + 96)
        sel_s[rows, 256:384] = sel_s[rows, 256:384] + moved(late, s2, 1, 0)

    def project(i, group):
        c = group * 4 + (y + i) % 4
        rows = pl.ds(pl.multiple_of(c * ROWS, ROWS), ROWS)
        qkv = dot(n_all[c], sel_s[...], 1, 0)
        q = (SCALE * qkv[:, 0:128]).astype(BF)
        k = qkv[:, 128:256].astype(BF)
        v = qkv[:, 256:384].astype(BF)
        kt = k.T
        vt = v.T
        for h in range(2):
            q_s[h, rows, :] = q[:, h * HD:h * HD + HD]
            k_s[h, rows, :] = k[:, h * HD:h * HD + HD]
            v_s[h, rows, :] = v[:, h * HD:h * HD + HD]
            kt_s[h, c] = kt[h * HD:h * HD + HD]
            vt_s[h, c] = vt[h * HD:h * HD + HD]
        return group

    lax.fori_loop(0, 4, project, xh)
    wait(n_on2)
    wait(n_cross)
    wait(n_cross2)
    lax.fori_loop(0, 4, project, 1 - xh)

    def sent(kind, c):
        rows = slice(*KINDS[kind])
        return remote(
            p_buf.at[c, rows], b_buf.at[d, rows], ps.at[kind, c], pr.at[kind, d], at(c, r)
        )

    def came(kind, c):
        rows = slice(*KINDS[kind])
        return remote(
            p_buf.at[c, rows], b_buf.at[c, rows], ps.at[kind, c], pr.at[kind, c], at(c, r)
        )

    def forward(h, c, k):
        q = q_s[h, pl.ds(pl.multiple_of(c * ROWS, ROWS), ROWS), :]
        m = jnp.full((8, ROWS), -jnp.inf, F32)
        for t in range(SEQ // TILE):
            ts = slice(t * TILE, t * TILE + TILE)
            s = dot(k_s[h, ts, :], q, 1, 1)
            p_s[ts, :] = s
            m = jnp.maximum(m, jnp.max(s.reshape(TILE // 8, 8, ROWS), axis=0))
        m = jnp.max(m, axis=0, keepdims=True)
        l = jnp.zeros((8, ROWS), F32)
        att = jnp.zeros((HD, ROWS), F32)
        for t in range(SEQ // TILE):
            e = jnp.exp(p_s[t * TILE:t * TILE + TILE, :] - m)
            l = l + jnp.sum(e.reshape(TILE // 8, 8, ROWS), axis=0)
            eb = e.astype(BF)
            e_s[k, t * TILE:t * TILE + TILE, :] = eb
            att += dot(vt_s[h, t], eb, 1, 0)
        l = jnp.sum(l, axis=0, keepdims=True)
        l = 1.0 / l
        p_buf[c, h * HD:h * HD + HD, :] = (att * l).astype(BF)
        r_s[k] = l
        pl.when(c != d)(lambda: sent(h, c).start())

    def forward_shared(i, _):
        forward(1, 4 * par + i, 8 + i)
        return 0

    def forward_own(i, _):
        forward(0, i, i)
        return 0

    lax.fori_loop(0, 4, forward_shared, 0)
    lax.fori_loop(0, 8, forward_own, 0)
    local = pltpu.make_async_copy(p_buf.at[d, 0:128], b_buf.at[d, 0:128], loc.at[0])
    local.start()
    wait(ca)

    def spread(c, _):
        rows = pl.ds(pl.multiple_of(c * ROWS, ROWS), ROWS)
        got = a_in[c]
        a_s[0, rows, :] = got[:, 0:HD]
        a_s[1, rows, :] = got[:, HD:2 * HD]
        return 0

    lax.fori_loop(0, ND, spread, 0)
    for s in range(3):
        wz3[s].wait()
        there = wl.at[:, :, :, z_from[s]]
        c = remote(there, there, ws.at[30 + s], wrs.at[30 + s], c_peer)
        c.start()
        wc3.append(c)

    def attend(h, c, k, base):
        rows = pl.ds(pl.multiple_of(c * ROWS, ROWS), ROWS)
        q = q_s[h, rows, :]
        a = a_s[h, rows, :]
        qt, at_ = q.T, a.T
        scale = r_s[k]
        delta = jnp.zeros((8, ROWS), F32)
        for t in range(SEQ // TILE):
            ts = slice(t * TILE, t * TILE + TILE)
            p = e_s[k, ts, :].astype(F32) * scale
            dp = dot(v_s[h, ts, :], a, 1, 1)
            dp_s[ts, :] = dp
            delta = delta + jnp.sum((p * dp).reshape(TILE // 8, 8, ROWS), axis=0)
        delta = jnp.sum(delta, axis=0, keepdims=True)
        dq = jnp.zeros((HD, ROWS), F32)
        for t in range(SEQ // TILE):
            ts = slice(t * TILE, t * TILE + TILE)
            p = e_s[k, ts, :].astype(F32) * scale
            pb = p.astype(BF)
            ds = (p * (dp_s[ts, :] - delta)).astype(BF)
            dq += dot(kt_s[h, t], ds, 1, 0)
            dk_s[:, ts] += dot(qt, ds, 1, 1)
            dv_s[:, ts] += dot(at_, pb, 1, 1)
        p_buf[c, base:base + HD, :] = (SCALE * dq).astype(BF)

    def totals(base, kind):
        for c in range(ND):
            cols = slice(c * ROWS, c * ROWS + ROWS)
            p_buf[c, base:base + HD, :] = dk_s[:, cols].astype(BF)
            p_buf[c, base + HD:base + 2 * HD, :] = dv_s[:, cols].astype(BF)
        for s in range(1, ND):
            sent(kind, (d + s) % ND).start()

    def attend_shared(i, _):
        c = 4 * par + i
        attend(1, c, 8 + i, 448)
        pl.when(c != d)(lambda: sent(5, c).start())
        return 0

    def attend_own(c, _):
        attend(0, c, c, 128)
        pl.when(c != d)(lambda: sent(2, c).start())
        return 0

    def grads(h):
        rows = slice(128, 320) if h == 0 else slice(320, 512)
        for t in range(3):
            cols = slice(256 * t, 256 * t + 256)
            total = dot(p_buf[0, rows], n_all[0, :, cols], 1, 0)
            for c in range(1, ND):
                total += dot(p_buf[c, rows], n_all[c, :, cols], 1, 0)
            gt_s[:, cols] = total.astype(BF)
        for b in range(2):
            rs[h, b] = moved(perm_g[b].reshape(512, E), gt_s[...], 1, 1).reshape(8, 64, 192)

    def to_core(h):
        out = [
            remote(rs.at[h, 1 - core, g], bc.at[h, g], gs.at[h, g], gr.at[h, g], c_peer) for g in range(8)
        ]
        start(out)
        return out

    def sum_cores(h, copies):
        for g in range(8):
            copies[g].wait()
            acc1[h, g] = (rs[h, core, g].astype(F32) + bc[h, g].astype(F32)).astype(BF)
        out = []
        for s in range(1, 8):
            to = (g0 + s) % 8
            out.append(remote(acc1.at[h, to], bz.at[h, g0], gs.at[h, 7 + s], gr.at[h, 7 + s], g_peers[s - 1]))
        start(out)
        return out

    def sum_up(h, copies):
        wait(copies)
        total = acc1[h, g0].astype(F32)
        for s in range(1, 8):
            total += bz[h, (g0 + s) % 8].astype(F32)
        acc3[h] = total
        out = []
        for s in range(1, ND):
            rows = pl.ds(pl.multiple_of(((d + s) % ND) * 8, 8), 8)
            out.append(
                remote(acc3.at[h, rows], finq.at[h, d], gs.at[h, 14 + s], gr.at[h, 14 + s], depth_peers[s - 1])
            )
        start(out)
        finq[h, d] = acc3[h, pl.ds(pl.multiple_of(d * 8, 8), 8), :]
        return out

    dk_s[...] = jnp.zeros_like(dk_s)
    dv_s[...] = jnp.zeros_like(dv_s)
    lax.fori_loop(0, 4, attend_shared, 0)
    totals(320, 4)
    grads(1)
    sc = to_core(1)

    local.wait()
    for s in range(1, ND):
        c = (d + s) % ND
        came(0, c).wait_recv()
        pl.when(c % 2 == half)(came(1, c).wait_recv)
    for k in range(4):
        t_s[0, 192 * k:192 * k + 64] = b_buf[2 * k, 0:64]
        t_s[0, 192 * k + 64:192 * k + 128] = b_buf[2 * k + half, 64:128]
        t_s[0, 192 * k + 128:192 * k + 192] = b_buf[2 * k + 1, 0:64]
    out_ref[...] = (x_ref[...].astype(F32) + dot(t_s[0].T, w_full[3], 1, 0)).astype(BF)
    out_copy = pltpu.make_async_copy(out_ref, out_hbm, loc.at[5])
    out_copy.start()
    go = dot(t_s[0], u_ref[...], 1, 0).astype(BF)
    for k in range(8):
        ro[k // 4, k % 4] = moved(perm_o[k], go, 1, 0)
    oc_copies = [
        remote(ro.at[1 - core, k], boc.at[k], os_.at[k], or_.at[k], c_peer) for k in range(4)
    ]
    start(oc_copies)

    dk_s[...] = jnp.zeros_like(dk_s)
    dv_s[...] = jnp.zeros_like(dv_s)
    lax.fori_loop(0, 2, attend_own, 0)
    for k in range(4):
        oc_copies[k].wait()
        oc[k] = (ro[core, k].astype(F32) + boc[k].astype(F32)).astype(BF)
    oz_copies = [
        remote(oc.at[(z + s) % 4], boz.at[s - 1], os_.at[3 + s], or_.at[3 + s], z_peers[s - 1])
        for s in range(1, 4)
    ]
    start(oz_copies)
    sz = sum_cores(1, sc)
    lax.fori_loop(2, 5, attend_own, 0)
    wait(oz_copies)
    total = (
        oc[z].astype(F32) + boz[0].astype(F32) + boz[1].astype(F32) + boz[2].astype(F32)
    )
    gap = jnp.zeros((2, E), F32)
    for q in range(4):
        parts = []
        for t in range(4):
            parts += [total[24 * q + 6 * t:24 * q + 6 * t + 6], gap]
        ox[q] = jnp.concatenate(parts, axis=0).astype(BF)
    x_to = [(1 - xh) * 2 + xl, xh * 2 + 1 - xl, (1 - xh) * 2 + 1 - xl]
    ox_copies = [
        remote(ox.at[x_to[s]], box.at[s], os_.at[7 + s], or_.at[7 + s], x_peers[s]) for s in range(3)
    ]
    start(ox_copies)
    lax.fori_loop(5, 7, attend_own, 0)
    wait(ox_copies)
    total = (
        ox[xh * 2 + xl].astype(F32) + box[0].astype(F32) + box[1].astype(F32) + box[2].astype(F32)
    )
    for t in range(4):
        oy[t] = total[8 * t:8 * t + 8]
    oy_copies = [
        remote(oy.at[(y + s) % 4], boy.at[s - 1], os_.at[9 + s], or_.at[9 + s], y_peers[s - 1])
        for s in range(1, 4)
    ]
    start(oy_copies)
    sd = sum_up(1, sz)
    lax.fori_loop(7, 8, attend_own, 0)
    totals(192, 3)
    local = pltpu.make_async_copy(p_buf.at[d, 128:512], b_buf.at[d, 128:512], loc.at[2])
    local.start()

    grads(0)
    cc = to_core(0)

    wait(wc3)
    for g in range(8):
        s1 = wl[g // 4, g % 4].reshape(256, E)
        s2 = wr[g // 4, g % 4].reshape(256, 384)
        rows = slice(96 * g, 96 * g + 96)
        w_full[0, rows] = moved(hot_s[0], s1, 1, 0)
        w_full[1, rows] = moved(hot_s[1], s1, 1, 0)
        w_full[2, rows] = moved(hot_s[2], s1, 1, 0)
        w_full[2, rows, 0:384] += moved(hot_s[3], s2, 1, 0)
        w_full[2, rows, 384:768] += moved(hot_s[4], s2, 1, 0)

    cz = sum_cores(0, cc)

    for s in range(1, ND):
        c = (d + s) % ND
        came(2, c).wait_recv()
        pl.when(c % 2 == half)(came(5, c).wait_recv)
    local.wait()
    for k in range(4):
        t_s[1, 192 * k:192 * k + 64] = b_buf[2 * k, 128:192]
        t_s[1, 192 * k + 64:192 * k + 128] = b_buf[2 * k + half, 448:512]
        t_s[1, 192 * k + 128:192 * k + 192] = b_buf[2 * k + 1, 128:192]
    dn = dot(t_s[1].T, w_full[0], 1, 1)
    last = sum_up(0, cz)

    for s in range(1, ND):
        c = (d + s) % ND
        for kind in (3, 4):
            came(kind, c).wait_recv()
    for k in range(4):
        lo, hi = 2 * k, 2 * k + 1
        for m in range(2):
            rows = slice(192 + 64 * m, 256 + 64 * m)
            t_s[2 + m, 192 * k:192 * k + 64] = b_buf[lo, rows]
            t_s[2 + m, 192 * k + 128:192 * k + 192] = b_buf[hi, rows]
            rows = slice(320 + 64 * m, 384 + 64 * m)
            t_s[2 + m, 192 * k + 64:192 * k + 128] = (
                b_buf[lo, rows].astype(F32) + b_buf[hi, rows].astype(F32)
            ).astype(BF)
    dn += dot(t_s[2].T, w_full[1], 1, 1)
    dn += dot(t_s[3].T, w_full[2], 1, 1)
    x = x_ref[...].astype(F32)
    centered = x - jnp.mean(x, axis=-1, keepdims=True)
    inverse = lax.rsqrt(jnp.mean(centered * centered, axis=-1, keepdims=True) + 1e-05)
    unit = centered * inverse
    du = dn * gain
    al_ref[...] = (
        u_ref[...].astype(F32)
        + inverse
        * (du - jnp.mean(du, axis=-1, keepdims=True) - unit * jnp.mean(du * unit, axis=-1, keepdims=True))
    ).astype(BF)

    al_copy = pltpu.make_async_copy(al_ref, al_hbm, loc.at[6])
    al_copy.start()

    wait(sd)
    wait(last)
    places = ((0, 128), (64, 0), (128, 64))
    dgain = jnp.zeros((6, 1), F32)
    for m, (g_ref, w_ref) in enumerate(((gq_ref, wq_ref), (gk_ref, wk_ref), (gv_ref, wv_ref))):
        own, sh = places[m]
        parts = []
        for k in range(4):
            parts.append(finq[0, 2 * k, 0:6, own:own + 64])
            parts.append(finq[1, 2 * k, 0:6, sh:sh + 64] + finq[1, 2 * k + 1, 0:6, sh:sh + 64])
            parts.append(finq[0, 2 * k + 1, 0:6, own:own + 64])
        g = jnp.concatenate(parts, axis=1)
        g_ref[...] = g
        dgain = dgain + jnp.sum(g * w_ref[...].astype(F32), axis=1, keepdims=True)
    wait(oy_copies)
    go_ref[...] = (oy[y] + boy[0] + boy[1] + boy[2])[0:6]
    F = lax.broadcasted_iota(jnp.int32, (6, E), 1)
    I = lax.broadcasted_iota(jnp.int32, (6, E), 0)
    own_gain = jnp.sum(
        jnp.where(F == 6 * (NR * d + r) + I, gain, 0.0), axis=1, keepdims=True
    )
    dg_ref[0:6] = jnp.broadcast_to(dgain / own_gain, (6, 128))
    dg_ref[6:8] = jnp.zeros((2, 128), F32)

    out_copy.wait()
    al_copy.wait()
    for s in range(1, ND):
        for kind in (0, 2, 3, 4):
            sent(kind, (d + s) % ND).wait_send()
    for i in range(4):
        c = 4 * par + i
        for kind in (1, 5):
            pl.when(c != d)(sent(kind, c).wait_send)


def fused(x, u, gain, wq, wk, wv, we):
    vm = pl.BlockSpec(memory_space=pltpu.VMEM)
    hbm = pl.BlockSpec(memory_space=pl.ANY)
    dma = lambda *shape: pltpu.SemaphoreType.DMA(shape)
    grad = jax.ShapeDtypeStruct((6, E), F32)
    return pl.pallas_call(
        kernel,
        out_shape=(
            jax.ShapeDtypeStruct((ROWS, E), BF),
            jax.ShapeDtypeStruct((ROWS, E), BF),
            grad, grad, grad, grad,
            jax.ShapeDtypeStruct((8, 128), F32),
        ),
        in_specs=[hbm] * 2 + [vm] * 5,
        out_specs=(hbm, hbm) + (vm,) * 5,
        scratch_shapes=[
            pltpu.VMEM((ROWS, E), BF),
            pltpu.VMEM((ROWS, E), BF),
            pltpu.VMEM((ROWS, E), BF),
            pltpu.VMEM((ROWS, E), BF),
            pltpu.VMEM((ND, ROWS, E), BF),
            pltpu.VMEM((2, 4, 2, 8, 16, E), BF),
            pltpu.VMEM((2, 4, 2, 8, 16, 384), BF),
            pltpu.VMEM((2, 4, 2, 8, 16, 256), BF),
            pltpu.VMEM((4, E, E), BF),
            pltpu.VMEM((7, 96, 256), BF),
            pltpu.VMEM((E, 384), BF),
            pltpu.VMEM((2, 8, 64, E), BF),
            pltpu.VMEM((8, 96, E), BF),
            pltpu.VMEM((2, SEQ, HD), BF),
            pltpu.VMEM((2, SEQ, HD), BF),
            pltpu.VMEM((2, SEQ, HD), BF),
            pltpu.VMEM((2, SEQ, HD), BF),
            pltpu.VMEM((2, ND, HD, ROWS), BF),
            pltpu.VMEM((2, ND, HD, ROWS), BF),
            pltpu.VMEM((ND, ROWS, 128), BF),
            pltpu.VMEM((ND, ROWS, 128), BF),
            pltpu.VMEM((12, SEQ, ROWS), BF),
            pltpu.VMEM((12, 1, ROWS), F32),
            pltpu.VMEM((SEQ, ROWS), F32),
            pltpu.VMEM((SEQ, ROWS), F32),
            pltpu.VMEM((HD, SEQ), F32),
            pltpu.VMEM((HD, SEQ), F32),
            pltpu.VMEM((ND, 512, ROWS), BF),
            pltpu.VMEM((ND, 512, ROWS), BF),
            pltpu.VMEM((192, E), BF),
            pltpu.VMEM((2, 2, 8, 64, 192), BF),
            pltpu.VMEM((2, 8, 64, 192), BF),
            pltpu.VMEM((2, 8, 64, 192), BF),
            pltpu.VMEM((2, 8, 64, 192), BF),
            pltpu.VMEM((2, 64, 192), F32),
            pltpu.VMEM((2, ND, 8, 192), F32),
            pltpu.VMEM((4, E, ROWS), BF),
            pltpu.VMEM((2, 4, 96, E), BF),
            pltpu.VMEM((4, 96, E), BF),
            pltpu.VMEM((4, 96, E), BF),
            pltpu.VMEM((3, 96, E), BF),
            pltpu.VMEM((4, 32, E), BF),
            pltpu.VMEM((3, 32, E), BF),
            pltpu.VMEM((4, 8, E), F32),
            pltpu.VMEM((3, 8, E), F32),
            dma(12), dma(12), dma(36), dma(36), dma(7), dma(7),
            dma(6, ND), dma(6, ND), dma(2, 22), dma(2, 22), dma(13), dma(13), dma(7),
        ],
        compiler_params=pltpu.CompilerParams(
            collective_id=1, has_side_effects=True, vmem_limit_bytes=VMEM_LIMIT
        ),
        name="fused",
    )(x, u, gain, wq, wk, wv, we)


def finish_kernel(*refs):
    for k in range(6):
        refs[7 + k][...] = refs[k][...]
    refs[13][...] = refs[6][...].T[0, 0:6]


def finish(arrays):
    vm = pl.BlockSpec(memory_space=pltpu.VMEM)
    return pl.pallas_call(
        finish_kernel,
        out_shape=tuple(jax.ShapeDtypeStruct(a.shape, a.dtype) for a in arrays[:6])
        + (jax.ShapeDtypeStruct((6,), F32),),
        in_specs=[vm] * 7,
        out_specs=(vm,) * 7,
        name="finish",
    )(*arrays)


def body(x, gain, wq, wk, wv, we, u):
    out, al, gq, gk, gv, go, dg = finish(
        fused(x.reshape(ROWS, E), u.reshape(ROWS, E), gain, wq, wk, wv, we)
    )
    return out.reshape(ROWS, 1, E), al.reshape(ROWS, 1, E), gq, gk, gv, go, dg


def solution(mesh):
    rows = P("depth", "res", None)
    shard = P(("depth", "res"), None)
    return jax.shard_map(
        body,
        mesh=mesh,
        in_specs=(rows, P(), shard, shard, shard, shard, rows),
        out_specs=(rows, rows, shard, shard, shard, shard, P(("depth", "res"))),
        check_vma=False,
    )
```

```python
import jax
import jax.numpy as jnp
from jax import lax
from jax.experimental import pallas as pl
from jax.experimental.pallas import tpu as pltpu
from jax.sharding import PartitionSpec as P

HD = 64
E = 768
ND = 8
NR = 16
ROWS = 256
SEQ = ND * ROWS
TILE = 256
SCALE = HD ** (-0.5)
MESH = pl.DeviceIdType.MESH
BF = jnp.bfloat16
F32 = jnp.float32
VMEM_LIMIT = 58 * 1024 * 1024


def place():
    d = lax.axis_index("depth")
    r = lax.axis_index("res")
    return d, r, d // 4, d % 4, r // 8, (r // 2) % 4, r % 2


def at(d, r):
    return {"depth": d, "res": r}


def barrier(peers):
    sem = pltpu.get_barrier_semaphore()
    for peer in peers:
        pl.semaphore_signal(sem, inc=1, device_id=peer, device_id_type=MESH)
    pl.semaphore_wait(sem, len(peers))


def remote(src, dst, send, recv, peer):
    return pltpu.make_async_remote_copy(
        src_ref=src, dst_ref=dst, send_sem=send, recv_sem=recv, device_id=peer, device_id_type=MESH
    )


def start(copies):
    for c in copies:
        c.start()


def wait(copies):
    for c in copies:
        c.wait()


def dot(a, b, ca, cb):
    return lax.dot_general(a, b, (((ca,), (cb,)), ((), ())), preferred_element_type=F32)


def hot(mask):
    return jnp.where(mask, 1.0, 0.0).astype(BF)


def moved(a, b, ca, cb):
    return dot(a, b, ca, cb).astype(BF)


SPLIT = 64
KINDS = ((0, 64), (64, 128), (128, 192), (192, 320), (320, 448), (448, 512))


def ring(full, d, xh, y, r, ss, rs):
    e = (d + 4) % ND
    across, up, down = at(e, r), at(xh * 4 + (y + 1) % 4, r), at(xh * 4 + (y + 3) % 4, r)
    lo, hi, far = xh * 4 + (y + 3) % 4, xh * 4 + (y + 1) % 4, xh * 4 + (y + 2) % 4
    mid = SPLIT + 96

    def send(k, peer, block, rows):
        return remote(full.at[block, rows], full.at[block, rows], ss.at[k], rs.at[k], peer)

    whole = slice(0, ROWS)
    c0 = send(0, across, d, whole)
    near = (send(1, up, d, whole), send(2, down, d, whole))
    near2 = (send(3, up, e, slice(SPLIT, ROWS)), send(4, down, e, slice(SPLIT, ROWS)))
    on = (send(5, up, lo, slice(0, 128)), send(6, down, hi, slice(128, ROWS)))
    cross = (send(7, across, lo, slice(0, SPLIT)), send(8, across, hi, slice(0, SPLIT)))
    cross2 = (send(9, across, far, slice(0, SPLIT)),)
    lo2, hi2 = (lo + 4) % ND, (hi + 4) % ND
    on2 = (send(10, up, lo2, slice(SPLIT, mid)), send(11, down, hi2, slice(mid, ROWS)))
    return c0, near, near2, on, cross, cross2, on2


def kernel(
    x_hbm, u_hbm, gain_ref, wq_ref, wk_ref, wv_ref, we_ref,
    out_hbm, al_hbm, gq_ref, gk_ref, gv_ref, go_ref, dg_ref,
    x_ref, u_ref, out_ref, al_ref, n_all, wl, wr, wc, w_full, hot_s, sel_s, perm_g, perm_o,
    q_s, k_s, v_s, a_s, kt_s, vt_s, a_out, a_in, e_s, r_s, p_s, dp_s, dk_s, dv_s,
    p_buf, b_buf, gt_s, rs, bc, acc1, bz, acc3, finq, t_s,
    ro, boc, oc, boz, ox, box, oy, boy,
    ns, nr, ws, wrs, as_, ar, ps, pr, gs, gr, os_, or_, loc,
):
    d, r, xh, y, xl, z, core = place()
    par, j, half = d % 2, d // 2, d // 4
    zc = z * 2 + core
    depth_peers = [at((d + s) % ND, r) for s in range(1, ND)]
    y_peers = [at(xh * 4 + (y + s) % 4, r) for s in range(1, 4)]
    x_peers = [at((1 - xh) * 4 + y, r), at(d, (1 - xl) * 8 + zc), at((1 - xh) * 4 + y, (1 - xl) * 8 + zc)]
    z_peers = [at(d, xl * 8 + ((z + s) % 4) * 2 + core) for s in range(1, 4)]
    z_from = [((z + 4 - s) % 4) * 2 + core for s in range(1, 4)]
    c_peer = at(d, xl * 8 + z * 2 + 1 - core)
    g0 = xl * 4 + z
    g_peers = [at(d, 2 * ((g0 + s) % 8) + core) for s in range(1, 8)]
    x_in = pltpu.make_async_copy(x_hbm, x_ref, loc.at[3])
    u_in = pltpu.make_async_copy(u_hbm, u_ref, loc.at[4])
    x_in.start()
    u_in.start()
    barrier(depth_peers + x_peers[2:] + g_peers + [c_peer])

    top = jnp.concatenate(
        [wq_ref[...].astype(F32), wk_ref[...].astype(F32), wv_ref[0:4].astype(F32)], axis=0
    )
    rest = jnp.concatenate([wv_ref[4:6].astype(F32), we_ref[...].astype(F32)], axis=0)
    rest = jnp.concatenate([rest[:, 0:384], rest[:, 384:768]], axis=0)
    wl[xh, y, xl, zc] = top.astype(BF)
    wr[xh, y, xl, zc] = rest.astype(BF)
    wy = []
    for s in range(3):
        for k, w in enumerate((wl, wr)):
            one = w.at[xh, y, xl, zc]
            wy.append(remote(one, one, ws.at[2 * s + k], wrs.at[2 * s + k], y_peers[s]))
    start(wy)

    x_in.wait()
    gain = gain_ref[...].reshape(1, E)
    x = x_ref[...].astype(F32)
    centered = x - jnp.mean(x, axis=-1, keepdims=True)
    inverse = lax.rsqrt(jnp.mean(centered * centered, axis=-1, keepdims=True) + 1e-05)
    n_all[d] = (centered * inverse * gain).astype(BF)
    n0, n_near, n_near2, n_on, n_cross, n_cross2, n_on2 = ring(n_all, d, xh, y, r, ns, nr)
    n0.start()

    window = pl.multiple_of(128 * ((3 * j) // 2), 128)
    offset = 192 * j - 128 * ((3 * j) // 2)
    other = pl.multiple_of(128 * ((3 * (2 * (1 - xh) + y // 2)) // 2), 128)
    wait(wy)
    start(n_near)
    windows = (other, window, other)
    wx = []
    for s in range(3):
        mine = wl.at[xh, :, xl, zc, :, pl.ds(windows[s], 256)]
        wx.append(remote(mine, wc.at[xh, :, xl, zc], ws.at[6 + 2 * s], wrs.at[6 + 2 * s], x_peers[s]))
        slab = wr.at[xh, :, xl, zc]
        wx.append(remote(slab, slab, ws.at[7 + 2 * s], wrs.at[7 + 2 * s], x_peers[s]))
    start(wx)
    own_w = pltpu.make_async_copy(
        wl.at[xh, :, xl, zc, :, pl.ds(window, 256)], wc.at[xh, :, xl, zc], loc.at[1]
    )
    own_w.start()
    R = lax.broadcasted_iota(jnp.int32, (96, 256), 0)
    K = lax.broadcasted_iota(jnp.int32, (96, 256), 1)
    o16, i6 = 16 * (R // 6), R % 6
    hot_s[0] = hot(K == o16 + i6)
    hot_s[1] = hot(K == o16 + 6 + i6)
    hot_s[2] = hot((K == o16 + 12 + i6) & (i6 < 4))
    hot_s[3] = hot((K == o16 + i6 - 4) & (i6 >= 4))
    hot_s[4] = hot((K == o16 + 8 + i6 - 4) & (i6 >= 4))
    hot_s[5] = hot(K == o16 + 2 + i6)
    hot_s[6] = hot(K == o16 + 10 + i6)
    K2 = lax.broadcasted_iota(jnp.int32, (256, 128), 0)
    C2 = lax.broadcasted_iota(jnp.int32, (256, 128), 1)
    pick = hot(K2 == jnp.where(C2 < 64, offset + 128 * par + C2, offset + C2))
    n0.wait()
    start(n_near2)
    wait(wx)
    own_w.wait()

    slab = wc.at[:, :, :, zc]
    wz1 = [remote(slab, slab, ws.at[12 + s], wrs.at[12 + s], z_peers[s]) for s in range(3)]
    start(wz1)
    wc1 = [remote(slab, slab, ws.at[15], wrs.at[15], c_peer)]
    start(wc1)
    slab = wr.at[:, :, :, zc]
    wz2 = [remote(slab, slab, ws.at[19 + s], wrs.at[19 + s], z_peers[s]) for s in range(3)]
    start(wz2)
    wc2 = [remote(slab, slab, ws.at[22], wrs.at[22], c_peer)]
    start(wc2)
    wait(n_near)
    start(n_on)
    start(n_cross)
    slab = wl.at[xh, :, xl, zc]
    wx2 = [remote(slab, slab, ws.at[33 + s], wrs.at[33 + s], x_peers[s]) for s in range(3)]
    start(wx2)
    p_buf[:, 448:512, :] = jnp.zeros((ND, 64, ROWS), BF)

    def orders(b, _):
        R = lax.broadcasted_iota(jnp.int32, (64, E), 0)
        F = lax.broadcasted_iota(jnp.int32, (64, E), 1)
        i = R % 8
        owner = 16 * ((R // 8) % 8) + 2 * (b % 8) + b // 8
        perm_g[b // 8, b % 8] = hot((F == 6 * owner + i) & (i < 6))
        return 0

    lax.fori_loop(0, NR, orders, 0)

    def orders_o(b, _):
        R = lax.broadcasted_iota(jnp.int32, (96, E), 0)
        F = lax.broadcasted_iota(jnp.int32, (96, E), 1)
        q = R // 24
        owner = (((q // 2) * 4 + (R // 6) % 4) * 2 + q % 2) * 8 + (b % 4) * 2 + b // 4
        perm_o[b] = hot(F == 6 * owner + R % 6)
        return 0

    lax.fori_loop(0, 8, orders_o, 0)

    for s in range(3):
        wz1[s].wait()
        there = wc.at[:, :, :, z_from[s]]
        c = remote(there, there, ws.at[16 + s], wrs.at[16 + s], c_peer)
        c.start()
        wc1.append(c)
    wait(n_near2)
    start(n_on2)
    wait(n_on)
    start(n_cross2)
    wait(wc1)

    for g in range(8):
        s1 = moved(wc[g // 4, g % 4].reshape(256, 256), pick, 1, 0)
        rows = slice(96 * g, 96 * g + 96)
        for m in range(3):
            sel_s[rows, 128 * m:128 * m + 128] = moved(hot_s[m], s1, 1, 0)

    for s in range(3):
        wz2[s].wait()
        there = wr.at[:, :, :, z_from[s]]
        c = remote(there, there, ws.at[23 + s], wrs.at[23 + s], c_peer)
        c.start()
        wc2.append(c)
    wait(wx2)
    slab = wl.at[:, :, :, zc]
    wz3 = [remote(slab, slab, ws.at[26 + s], wrs.at[26 + s], z_peers[s]) for s in range(3)]
    start(wz3)
    wc3 = [remote(slab, slab, ws.at[29], wrs.at[29], c_peer)]
    start(wc3)
    wait(wc2)
    u_in.wait()
    for g in range(8):
        s2 = wr[g // 4, g % 4].reshape(256, 384)
        rows = slice(96 * g, 96 * g + 96)
        w_full[3, rows, 0:384] = moved(hot_s[5], s2, 1, 0)
        w_full[3, rows, 384:768] = moved(hot_s[6], s2, 1, 0)
    a = dot(u_ref[...], w_full[3], 1, 1).astype(BF)
    for t in range(ND):
        own, sh = 192 * (t // 2) + 128 * (t % 2), 192 * (t // 2) + 64
        a_out[t] = jnp.concatenate([a[:, own:own + HD], a[:, sh:sh + HD]], axis=1)
    ca = []
    for s in range(1, ND):
        c = remote(a_out.at[(d + s) % ND], a_in.at[d], as_.at[s - 1], ar.at[s - 1], depth_peers[s - 1])
        c.start()
        ca.append(c)
    a_in[d] = a_out[d]

    inner = pl.multiple_of(128 * ((3 * j) // 2) - 384 * half, 128)
    for g in range(8):
        s2 = moved(wr[g // 4, g % 4, :, :, :, pl.ds(inner, 256)].reshape(256, 256), pick, 1, 0)
        late = jnp.where(half == 0, hot_s[3], hot_s[4])
        rows = slice(96 * g, 96 * g + 96)
        sel_s[rows, 256:384] = sel_s[rows, 256:384] + moved(late, s2, 1, 0)

    def project(i, group):
        c = group * 4 + (y + i) % 4
        rows = pl.ds(pl.multiple_of(c * ROWS, ROWS), ROWS)
        qkv = dot(n_all[c], sel_s[...], 1, 0)
        q = (SCALE * qkv[:, 0:128]).astype(BF)
        k = qkv[:, 128:256].astype(BF)
        v = qkv[:, 256:384].astype(BF)
        kt = k.T
        vt = v.T
        for h in range(2):
            q_s[h, rows, :] = q[:, h * HD:h * HD + HD]
            k_s[h, rows, :] = k[:, h * HD:h * HD + HD]
            v_s[h, rows, :] = v[:, h * HD:h * HD + HD]
            kt_s[h, c] = kt[h * HD:h * HD + HD]
            vt_s[h, c] = vt[h * HD:h * HD + HD]
        return group

    lax.fori_loop(0, 4, project, xh)
    wait(n_on2)
    wait(n_cross)
    wait(n_cross2)
    lax.fori_loop(0, 4, project, 1 - xh)

    def sent(kind, c):
        rows = slice(*KINDS[kind])
        return remote(
            p_buf.at[c, rows], b_buf.at[d, rows], ps.at[kind, c], pr.at[kind, d], at(c, r)
        )

    def came(kind, c):
        rows = slice(*KINDS[kind])
        return remote(
            p_buf.at[c, rows], b_buf.at[c, rows], ps.at[kind, c], pr.at[kind, c], at(c, r)
        )

    def forward(h, c, k):
        q = q_s[h, pl.ds(pl.multiple_of(c * ROWS, ROWS), ROWS), :]
        m = jnp.full((8, ROWS), -jnp.inf, F32)
        for t in range(SEQ // TILE):
            ts = slice(t * TILE, t * TILE + TILE)
            s = dot(k_s[h, ts, :], q, 1, 1)
            p_s[ts, :] = s
            m = jnp.maximum(m, jnp.max(s.reshape(TILE // 8, 8, ROWS), axis=0))
        m = jnp.max(m, axis=0, keepdims=True)
        l = jnp.zeros((8, ROWS), F32)
        att = jnp.zeros((HD, ROWS), F32)
        for t in range(SEQ // TILE):
            e = jnp.exp(p_s[t * TILE:t * TILE + TILE, :] - m)
            eb = e.astype(BF)
            l = l + jnp.sum(eb.astype(F32).reshape(TILE // 8, 8, ROWS), axis=0)
            e_s[k, t * TILE:t * TILE + TILE, :] = eb
            att += dot(vt_s[h, t], eb, 1, 0)
        l = jnp.sum(l, axis=0, keepdims=True)
        l = 1.0 / l
        p_buf[c, h * HD:h * HD + HD, :] = (att * l).astype(BF)
        r_s[k] = l
        pl.when(c != d)(lambda: sent(h, c).start())

    def forward_shared(i, _):
        forward(1, 4 * par + i, 8 + i)
        return 0

    def forward_own(i, _):
        forward(0, i, i)
        return 0

    lax.fori_loop(0, 4, forward_shared, 0)
    lax.fori_loop(0, 8, forward_own, 0)
    local = pltpu.make_async_copy(p_buf.at[d, 0:128], b_buf.at[d, 0:128], loc.at[0])
    local.start()
    wait(ca)

    def spread(c, _):
        rows = pl.ds(pl.multiple_of(c * ROWS, ROWS), ROWS)
        got = a_in[c]
        a_s[0, rows, :] = got[:, 0:HD]
        a_s[1, rows, :] = got[:, HD:2 * HD]
        return 0

    lax.fori_loop(0, ND, spread, 0)
    for s in range(3):
        wz3[s].wait()
        there = wl.at[:, :, :, z_from[s]]
        c = remote(there, there, ws.at[30 + s], wrs.at[30 + s], c_peer)
        c.start()
        wc3.append(c)

    def attend(h, c, k, base):
        rows = pl.ds(pl.multiple_of(c * ROWS, ROWS), ROWS)
        q = q_s[h, rows, :]
        a = a_s[h, rows, :]
        qt, at_ = q.T, a.T
        scale = r_s[k]
        delta = jnp.zeros((8, ROWS), F32)
        for t in range(SEQ // TILE):
            ts = slice(t * TILE, t * TILE + TILE)
            p = e_s[k, ts, :].astype(F32) * scale
            dp = dot(v_s[h, ts, :], a, 1, 1)
            dp_s[ts, :] = dp
            delta = delta + jnp.sum((p * dp).reshape(TILE // 8, 8, ROWS), axis=0)
        delta = jnp.sum(delta, axis=0, keepdims=True)
        dq = jnp.zeros((HD, ROWS), F32)
        for t in range(SEQ // TILE):
            ts = slice(t * TILE, t * TILE + TILE)
            p = e_s[k, ts, :].astype(F32) * scale
            pb = p.astype(BF)
            ds = (p * (dp_s[ts, :] - delta)).astype(BF)
            dq += dot(kt_s[h, t], ds, 1, 0)
            dk_s[:, ts] += dot(qt, ds, 1, 1)
            dv_s[:, ts] += dot(at_, pb, 1, 1)
        p_buf[c, base:base + HD, :] = (SCALE * dq).astype(BF)

    def totals(base, kind):
        for c in range(ND):
            cols = slice(c * ROWS, c * ROWS + ROWS)
            p_buf[c, base:base + HD, :] = dk_s[:, cols].astype(BF)
            p_buf[c, base + HD:base + 2 * HD, :] = dv_s[:, cols].astype(BF)
        for s in range(1, ND):
            sent(kind, (d + s) % ND).start()

    def attend_shared(i, _):
        c = 4 * par + i
        attend(1, c, 8 + i, 448)
        pl.when(c != d)(lambda: sent(5, c).start())
        return 0

    def attend_own(c, _):
        attend(0, c, c, 128)
        pl.when(c != d)(lambda: sent(2, c).start())
        return 0

    def grads(h):
        rows = slice(128, 320) if h == 0 else slice(320, 512)
        for t in range(3):
            cols = slice(256 * t, 256 * t + 256)
            total = dot(p_buf[0, rows], n_all[0, :, cols], 1, 0)
            for c in range(1, ND):
                total += dot(p_buf[c, rows], n_all[c, :, cols], 1, 0)
            gt_s[:, cols] = total.astype(BF)
        for b in range(2):
            rs[h, b] = moved(perm_g[b].reshape(512, E), gt_s[...], 1, 1).reshape(8, 64, 192)

    def to_core(h):
        out = [
            remote(rs.at[h, 1 - core, g], bc.at[h, g], gs.at[h, g], gr.at[h, g], c_peer) for g in range(8)
        ]
        start(out)
        return out

    def sum_cores(h, copies):
        for g in range(8):
            copies[g].wait()
            acc1[h, g] = (rs[h, core, g].astype(F32) + bc[h, g].astype(F32)).astype(BF)
        out = []
        for s in range(1, 8):
            to = (g0 + s) % 8
            out.append(remote(acc1.at[h, to], bz.at[h, g0], gs.at[h, 7 + s], gr.at[h, 7 + s], g_peers[s - 1]))
        start(out)
        return out

    def sum_up(h, copies):
        wait(copies)
        total = acc1[h, g0].astype(F32)
        for s in range(1, 8):
            total += bz[h, (g0 + s) % 8].astype(F32)
        acc3[h] = total
        out = []
        for s in range(1, ND):
            rows = pl.ds(pl.multiple_of(((d + s) % ND) * 8, 8), 8)
            out.append(
                remote(acc3.at[h, rows], finq.at[h, d], gs.at[h, 14 + s], gr.at[h, 14 + s], depth_peers[s - 1])
            )
        start(out)
        finq[h, d] = acc3[h, pl.ds(pl.multiple_of(d * 8, 8), 8), :]
        return out

    dk_s[...] = jnp.zeros_like(dk_s)
    dv_s[...] = jnp.zeros_like(dv_s)
    lax.fori_loop(0, 4, attend_shared, 0)
    totals(320, 4)
    grads(1)
    sc = to_core(1)

    local.wait()
    for s in range(1, ND):
        c = (d + s) % ND
        came(0, c).wait_recv()
        pl.when(c % 2 == half)(came(1, c).wait_recv)
    for k in range(4):
        t_s[0, 192 * k:192 * k + 64] = b_buf[2 * k, 0:64]
        t_s[0, 192 * k + 64:192 * k + 128] = b_buf[2 * k + half, 64:128]
        t_s[0, 192 * k + 128:192 * k + 192] = b_buf[2 * k + 1, 0:64]
    out_ref[...] = (x_ref[...].astype(F32) + dot(t_s[0].T, w_full[3], 1, 0)).astype(BF)
    out_copy = pltpu.make_async_copy(out_ref, out_hbm, loc.at[5])
    out_copy.start()
    go = dot(t_s[0], u_ref[...], 1, 0).astype(BF)
    for k in range(8):
        ro[k // 4, k % 4] = moved(perm_o[k], go, 1, 0)
    oc_copies = [
        remote(ro.at[1 - core, k], boc.at[k], os_.at[k], or_.at[k], c_peer) for k in range(4)
    ]
    start(oc_copies)

    dk_s[...] = jnp.zeros_like(dk_s)
    dv_s[...] = jnp.zeros_like(dv_s)
    lax.fori_loop(0, 2, attend_own, 0)
    for k in range(4):
        oc_copies[k].wait()
        oc[k] = (ro[core, k].astype(F32) + boc[k].astype(F32)).astype(BF)
    oz_copies = [
        remote(oc.at[(z + s) % 4], boz.at[s - 1], os_.at[3 + s], or_.at[3 + s], z_peers[s - 1])
        for s in range(1, 4)
    ]
    start(oz_copies)
    sz = sum_cores(1, sc)
    lax.fori_loop(2, 5, attend_own, 0)
    wait(oz_copies)
    total = (
        oc[z].astype(F32) + boz[0].astype(F32) + boz[1].astype(F32) + boz[2].astype(F32)
    )
    gap = jnp.zeros((2, E), F32)
    for q in range(4):
        parts = []
        for t in range(4):
            parts += [total[24 * q + 6 * t:24 * q + 6 * t + 6], gap]
        ox[q] = jnp.concatenate(parts, axis=0).astype(BF)
    x_to = [(1 - xh) * 2 + xl, xh * 2 + 1 - xl, (1 - xh) * 2 + 1 - xl]
    ox_copies = [
        remote(ox.at[x_to[s]], box.at[s], os_.at[7 + s], or_.at[7 + s], x_peers[s]) for s in range(3)
    ]
    start(ox_copies)
    lax.fori_loop(5, 7, attend_own, 0)
    wait(ox_copies)
    total = (
        ox[xh * 2 + xl].astype(F32) + box[0].astype(F32) + box[1].astype(F32) + box[2].astype(F32)
    )
    for t in range(4):
        oy[t] = total[8 * t:8 * t + 8]
    oy_copies = [
        remote(oy.at[(y + s) % 4], boy.at[s - 1], os_.at[9 + s], or_.at[9 + s], y_peers[s - 1])
        for s in range(1, 4)
    ]
    start(oy_copies)
    sd = sum_up(1, sz)
    lax.fori_loop(7, 8, attend_own, 0)
    totals(192, 3)
    local = pltpu.make_async_copy(p_buf.at[d, 128:512], b_buf.at[d, 128:512], loc.at[2])
    local.start()

    grads(0)
    cc = to_core(0)

    wait(wc3)
    for g in range(8):
        s1 = wl[g // 4, g % 4].reshape(256, E)
        s2 = wr[g // 4, g % 4].reshape(256, 384)
        rows = slice(96 * g, 96 * g + 96)
        w_full[0, rows] = moved(hot_s[0], s1, 1, 0)
        w_full[1, rows] = moved(hot_s[1], s1, 1, 0)
        w_full[2, rows] = moved(hot_s[2], s1, 1, 0)
        w_full[2, rows, 0:384] += moved(hot_s[3], s2, 1, 0)
        w_full[2, rows, 384:768] += moved(hot_s[4], s2, 1, 0)

    cz = sum_cores(0, cc)

    for s in range(1, ND):
        c = (d + s) % ND
        came(2, c).wait_recv()
        pl.when(c % 2 == half)(came(5, c).wait_recv)
    local.wait()
    for k in range(4):
        t_s[1, 192 * k:192 * k + 64] = b_buf[2 * k, 128:192]
        t_s[1, 192 * k + 64:192 * k + 128] = b_buf[2 * k + half, 448:512]
        t_s[1, 192 * k + 128:192 * k + 192] = b_buf[2 * k + 1, 128:192]
    dn = dot(t_s[1].T, w_full[0], 1, 1)
    last = sum_up(0, cz)

    for s in range(1, ND):
        c = (d + s) % ND
        for kind in (3, 4):
            came(kind, c).wait_recv()
    for k in range(4):
        lo, hi = 2 * k, 2 * k + 1
        for m in range(2):
            rows = slice(192 + 64 * m, 256 + 64 * m)
            t_s[2 + m, 192 * k:192 * k + 64] = b_buf[lo, rows]
            t_s[2 + m, 192 * k + 128:192 * k + 192] = b_buf[hi, rows]
            rows = slice(320 + 64 * m, 384 + 64 * m)
            t_s[2 + m, 192 * k + 64:192 * k + 128] = (
                b_buf[lo, rows].astype(F32) + b_buf[hi, rows].astype(F32)
            ).astype(BF)
    dn += dot(t_s[2].T, w_full[1], 1, 1)
    dn += dot(t_s[3].T, w_full[2], 1, 1)
    x = x_ref[...].astype(F32)
    centered = x - jnp.mean(x, axis=-1, keepdims=True)
    inverse = lax.rsqrt(jnp.mean(centered * centered, axis=-1, keepdims=True) + 1e-05)
    unit = centered * inverse
    du = dn * gain
    al_ref[...] = (
        u_ref[...].astype(F32)
        + inverse
        * (du - jnp.mean(du, axis=-1, keepdims=True) - unit * jnp.mean(du * unit, axis=-1, keepdims=True))
    ).astype(BF)

    al_copy = pltpu.make_async_copy(al_ref, al_hbm, loc.at[6])
    al_copy.start()

    wait(sd)
    wait(last)
    places = ((0, 128), (64, 0), (128, 64))
    dgain = jnp.zeros((6, 1), F32)
    for m, (g_ref, w_ref) in enumerate(((gq_ref, wq_ref), (gk_ref, wk_ref), (gv_ref, wv_ref))):
        own, sh = places[m]
        parts = []
        for k in range(4):
            parts.append(finq[0, 2 * k, 0:6, own:own + 64])
            parts.append(finq[1, 2 * k, 0:6, sh:sh + 64] + finq[1, 2 * k + 1, 0:6, sh:sh + 64])
            parts.append(finq[0, 2 * k + 1, 0:6, own:own + 64])
        g = jnp.concatenate(parts, axis=1)
        g_ref[...] = g
        dgain = dgain + jnp.sum(g * w_ref[...].astype(F32), axis=1, keepdims=True)
    wait(oy_copies)
    go_ref[...] = (oy[y] + boy[0] + boy[1] + boy[2])[0:6]
    F = lax.broadcasted_iota(jnp.int32, (6, E), 1)
    I = lax.broadcasted_iota(jnp.int32, (6, E), 0)
    own_gain = jnp.sum(
        jnp.where(F == 6 * (NR * d + r) + I, gain, 0.0), axis=1, keepdims=True
    )
    dg_ref[0:6] = jnp.broadcast_to(dgain / own_gain, (6, 128))
    dg_ref[6:8] = jnp.zeros((2, 128), F32)

    out_copy.wait()
    al_copy.wait()
    for s in range(1, ND):
        for kind in (0, 2, 3, 4):
            sent(kind, (d + s) % ND).wait_send()
    for i in range(4):
        c = 4 * par + i
        for kind in (1, 5):
            pl.when(c != d)(sent(kind, c).wait_send)


def fused(x, u, gain, wq, wk, wv, we):
    vm = pl.BlockSpec(memory_space=pltpu.VMEM)
    hbm = pl.BlockSpec(memory_space=pl.ANY)
    dma = lambda *shape: pltpu.SemaphoreType.DMA(shape)
    grad = jax.ShapeDtypeStruct((6, E), F32)
    return pl.pallas_call(
        kernel,
        out_shape=(
            jax.ShapeDtypeStruct((ROWS, E), BF),
            jax.ShapeDtypeStruct((ROWS, E), BF),
            grad, grad, grad, grad,
            jax.ShapeDtypeStruct((8, 128), F32),
        ),
        in_specs=[hbm] * 2 + [vm] * 5,
        out_specs=(hbm, hbm) + (vm,) * 5,
        scratch_shapes=[
            pltpu.VMEM((ROWS, E), BF),
            pltpu.VMEM((ROWS, E), BF),
            pltpu.VMEM((ROWS, E), BF),
            pltpu.VMEM((ROWS, E), BF),
            pltpu.VMEM((ND, ROWS, E), BF),
            pltpu.VMEM((2, 4, 2, 8, 16, E), BF),
            pltpu.VMEM((2, 4, 2, 8, 16, 384), BF),
            pltpu.VMEM((2, 4, 2, 8, 16, 256), BF),
            pltpu.VMEM((4, E, E), BF),
            pltpu.VMEM((7, 96, 256), BF),
            pltpu.VMEM((E, 384), BF),
            pltpu.VMEM((2, 8, 64, E), BF),
            pltpu.VMEM((8, 96, E), BF),
            pltpu.VMEM((2, SEQ, HD), BF),
            pltpu.VMEM((2, SEQ, HD), BF),
            pltpu.VMEM((2, SEQ, HD), BF),
            pltpu.VMEM((2, SEQ, HD), BF),
            pltpu.VMEM((2, ND, HD, ROWS), BF),
            pltpu.VMEM((2, ND, HD, ROWS), BF),
            pltpu.VMEM((ND, ROWS, 128), BF),
            pltpu.VMEM((ND, ROWS, 128), BF),
            pltpu.VMEM((12, SEQ, ROWS), BF),
            pltpu.VMEM((12, 1, ROWS), F32),
            pltpu.VMEM((SEQ, ROWS), F32),
            pltpu.VMEM((SEQ, ROWS), F32),
            pltpu.VMEM((HD, SEQ), F32),
            pltpu.VMEM((HD, SEQ), F32),
            pltpu.VMEM((ND, 512, ROWS), BF),
            pltpu.VMEM((ND, 512, ROWS), BF),
            pltpu.VMEM((192, E), BF),
            pltpu.VMEM((2, 2, 8, 64, 192), BF),
            pltpu.VMEM((2, 8, 64, 192), BF),
            pltpu.VMEM((2, 8, 64, 192), BF),
            pltpu.VMEM((2, 8, 64, 192), BF),
            pltpu.VMEM((2, 64, 192), F32),
            pltpu.VMEM((2, ND, 8, 192), F32),
            pltpu.VMEM((4, E, ROWS), BF),
            pltpu.VMEM((2, 4, 96, E), BF),
            pltpu.VMEM((4, 96, E), BF),
            pltpu.VMEM((4, 96, E), BF),
            pltpu.VMEM((3, 96, E), BF),
            pltpu.VMEM((4, 32, E), BF),
            pltpu.VMEM((3, 32, E), BF),
            pltpu.VMEM((4, 8, E), F32),
            pltpu.VMEM((3, 8, E), F32),
            dma(12), dma(12), dma(36), dma(36), dma(7), dma(7),
            dma(6, ND), dma(6, ND), dma(2, 22), dma(2, 22), dma(13), dma(13), dma(7),
        ],
        compiler_params=pltpu.CompilerParams(
            collective_id=1, has_side_effects=True, vmem_limit_bytes=VMEM_LIMIT
        ),
        name="fused",
    )(x, u, gain, wq, wk, wv, we)


def finish_kernel(*refs):
    for k in range(6):
        refs[7 + k][...] = refs[k][...]
    refs[13][...] = refs[6][...].T[0, 0:6]


def finish(arrays):
    vm = pl.BlockSpec(memory_space=pltpu.VMEM)
    return pl.pallas_call(
        finish_kernel,
        out_shape=tuple(jax.ShapeDtypeStruct(a.shape, a.dtype) for a in arrays[:6])
        + (jax.ShapeDtypeStruct((6,), F32),),
        in_specs=[vm] * 7,
        out_specs=(vm,) * 7,
        name="finish",
    )(*arrays)


def body(x, gain, wq, wk, wv, we, u):
    out, al, gq, gk, gv, go, dg = finish(
        fused(x.reshape(ROWS, E), u.reshape(ROWS, E), gain, wq, wk, wv, we)
    )
    return out.reshape(ROWS, 1, E), al.reshape(ROWS, 1, E), gq, gk, gv, go, dg


def solution(mesh):
    rows = P("depth", "res", None)
    shard = P(("depth", "res"), None)
    return jax.shard_map(
        body,
        mesh=mesh,
        in_specs=(rows, P(), shard, shard, shard, shard, rows),
        out_specs=(rows, rows, shard, shard, shard, shard, P(("depth", "res"))),
        check_vma=False,
    )
```
